256 devices in a mesh: rack: 4 (over x), outer: 16 (over z, core), tp: 4 (over y).
Axes of the slice: x: 4, y: 4, z: 8, core: 2. Of those that a mesh axis runs over, the one named last changes fastest.
Arguments:
- context: bfloat16 [65536, 6144], P(('rack', 'outer'), 'tp'), may hold values from -0.8 to 0.8
- cotangent: bfloat16 [65536, 3072], P(('rack', 'outer')), may hold values from -40 to 40
Outputs:
- merged_grad: bfloat16 [3072, 6144], P(('rack', 'outer'), 'tp')
The draws below stay inside these ranges and needn't reach their ends.
All inputs are finite; a program needn't handle non-finite values.
Results may differ from the reference program's by a relative error of at most 0.015.
Values may be sent and summed in bfloat16 or wider, within the bound.
A program may use at most 64 MiB of HBM per device.

```python
import math
import jax
import jax.numpy as jnp
from jax import lax

D = 6144
COLS = 3072
TOK = 1024
REPLICAS = 64
TOKENS = 65536
LEVELS = 4
N_RACK = 4
N_OUTER = 16


def draw_context(key, part):
    key = jax.random.fold_in(key, 11)
    key_common, key_noise, key_cols = jax.random.split(key, 3)
    column_pos = jnp.arange(D).astype(jnp.float32) / max(D - 1, 1)
    common = jnp.clip(jax.random.normal(key_common, (TOK, D), jnp.float32), -6.0, 6.0)
    noise = jnp.clip(jax.random.normal(key_noise, (TOKENS, D), jnp.float32), -6.0, 6.0)
    share = 0.3 + 0.6 * column_pos
    col_scale = jnp.exp(jax.random.uniform(key_cols, (D,), jnp.float32, math.log(0.3), math.log(3.0)))
    values = share[None, :] * jnp.tile(common, (REPLICAS, 1)) + jnp.sqrt(1.0 - share * share)[None, :] * noise
    values = values * col_scale[None, :] * (1.0 / 32.0)
    return values.astype(jnp.bfloat16)


def draw_cotangent(key, part):
    key = jax.random.fold_in(key, 23)
    key_common, key_noise, key_scale = jax.random.split(key, 3)
    ramp_pos = jnp.arange(COLS).astype(jnp.float32) / max(COLS - 1, 1)
    common = jnp.clip(jax.random.normal(key_common, (TOK, COLS), jnp.float32), -6.0, 6.0)
    noise = jnp.clip(jax.random.normal(key_noise, (TOKENS, COLS), jnp.float32), -6.0, 6.0)
    share = 0.3 + 0.6 * ramp_pos
    col_scale = jnp.exp(math.log(3.0) * ramp_pos)
    replica_scale = jnp.exp(jax.random.uniform(key_scale, (REPLICAS,), jnp.float32, math.log(0.5), math.log(1.5)))
    row_scale = jnp.repeat(replica_scale, TOK)
    values = share[None, :] * jnp.tile(common, (REPLICAS, 1)) + jnp.sqrt(1.0 - share * share)[None, :] * noise
    values = values * row_scale[:, None] * col_scale[None, :]
    return values.astype(jnp.bfloat16)


def setup_inputs(seed: int = 0) -> dict:
    keys = jax.random.split(jax.random.key(seed), 3)
    context = draw_context(jax.random.fold_in(keys[2], 71), 0)
    cotangent = draw_cotangent(jax.random.fold_in(keys[2], 71), 0)
    return {"context": context, "cotangent": cotangent}


EPS = 1e-6


def combine_pair(first, second):
    ab = jnp.sum(first * second)
    aa = jnp.sum(first * first)
    bb = jnp.sum(second * second)
    mixed = (1.0 - ab / (2.0 * (aa + EPS))) * first + (1.0 - ab / (2.0 * (bb + EPS))) * second
    return mixed.astype(jnp.bfloat16)


def reference(context, cotangent):
    merged = []
    for outer_pos in range(N_OUTER):
        def add_rack(rack_pos, total):
            start = jnp.asarray((rack_pos * N_OUTER + outer_pos) * TOK).astype(jnp.int32)
            rows_x = lax.dynamic_slice_in_dim(context, start, TOK, 0)
            rows_g = lax.dynamic_slice_in_dim(cotangent, start, TOK, 0)
            term = lax.dot_general(rows_g, rows_x, (((0,), (0,)), ((), ())), preferred_element_type=jnp.float32)
            term = lax.optimization_barrier(term.astype(jnp.bfloat16)).astype(jnp.float32)
            return total + term
        total = lax.fori_loop(0, N_RACK, add_rack, jnp.zeros((COLS, D), jnp.float32))
        merged.append(total.astype(jnp.bfloat16))
    for level in range(LEVELS):
        renewed = []
        for outer_pos in range(N_OUTER):
            first = merged[outer_pos].astype(jnp.float32)
            second = merged[outer_pos ^ (1 << level)].astype(jnp.float32)
            renewed.append(combine_pair(first, second))
        merged = renewed
    return merged[0]
```

```python
import functools
import jax
import jax.numpy as jnp
from jax import lax
from jax.experimental import pallas as pl
from jax.experimental.pallas import tpu as pltpu
from jax.sharding import PartitionSpec as P

EPS = 1e-06
MESH = pl.DeviceIdType.MESH
F32 = jnp.float32
BF16 = jnp.bfloat16


def xor_roll(x, distance, axis, index, size):
    up = pltpu.roll(x, x.shape[axis] - distance, axis)
    down = pltpu.roll(x, distance, axis)
    return jnp.where((index & distance) == 0, up, down)


def merge_weights(gram, n, levels):
    row = lax.broadcasted_iota(jnp.int32, gram.shape, 0)
    lane = lax.broadcasted_iota(jnp.int32, gram.shape, 1)
    diagonal = row == lane
    weights_t = jnp.where(diagonal, 1.0, 0.0).astype(F32)

    def mixing(aa, bb, ab):
        aa, bb = jnp.maximum(aa, 0.0), jnp.maximum(bb, 0.0)
        bound = jnp.sqrt(aa) * jnp.sqrt(bb)
        ab = jnp.clip(ab, -bound, bound)
        return 1.0 - ab / (2.0 * (aa + EPS)), 1.0 - ab / (2.0 * (bb + EPS))

    for level in range(levels):
        d = 1 << level
        partner = (row ^ d) == lane
        gram_r = xor_roll(gram, d, 0, row, n)
        gram_l = xor_roll(gram, d, 1, lane, n)

        def column(x, mask):
            return jnp.sum(jnp.where(mask, x, 0.0), axis=1, keepdims=True)

        def line(x, mask):
            return jnp.sum(jnp.where(mask, x, 0.0), axis=0, keepdims=True)

        ca, cb = mixing(column(gram, diagonal), column(gram_r, partner), column(gram, partner))
        ra, rb = mixing(line(gram, diagonal), line(gram_l, partner), line(gram, partner))
        mixed = ca * gram + cb * gram_r
        gram = ra * mixed + rb * xor_roll(mixed, d, 1, lane, n)
        weights_t = ra * weights_t + rb * xor_roll(weights_t, d, 1, lane, n)
    return weights_t[:, 0:1]


def kernel(ctx_hbm, cot_hbm, out_ref, ctx, cot, cot_t, p, xr, blocks, pairs, g1, g2,
           load_sem, xs_sem, xr_sem, as_sem, ar_sem, gs_sem, gr_sem):
    n_rack, n_outer, n_tp = lax.axis_size("rack"), lax.axis_size("outer"), lax.axis_size("tp")
    k, o, t = lax.axis_index("rack"), lax.axis_index("outer"), lax.axis_index("tp")
    left, right, opp = (k + 3) % 4, (k + 1) % 4, (k + 2) % 4
    z, core = o // 2, o % 2
    zh, zl = z // 4, z % 4
    tok, width = ctx.shape
    half = width // 2
    rack_rows = p.shape[0] // 4
    rows48 = rack_rows // 16
    step_rows = 2 * rows48
    unit_rows = rack_rows // 2
    dest = (opp, right, left, k)

    barrier = pltpu.get_barrier_semaphore()
    for d in range(1, n_rack * n_tp):
        dk, dt = d // n_tp, d % n_tp
        pl.semaphore_signal(
            barrier, inc=1,
            device_id={"rack": (k + dk) % n_rack, "tp": (t + dt) % n_tp}, device_id_type=MESH)
    for d in range(1, n_outer):
        pl.semaphore_signal(
            barrier, inc=1, device_id={"outer": (o + d) % n_outer}, device_id_type=MESH)

    def target(s):
        return (zh ^ (1 - s // 4)) * 4 + (zl + s + s // 4) % 4

    def source(s):
        return (zh ^ (1 - s // 4)) * 4 + (zl + 8 - s - s // 4) % 4

    def unit_cols(u):
        h = zh ^ (1 - u // 4)
        return dest[u % 4] * rack_rows + h * unit_rows

    def cot_load(u):
        cols = pl.ds(pl.multiple_of(unit_cols(u), 128), unit_rows)
        return pltpu.make_async_copy(cot_hbm.at[:, cols], cot.at[u], load_sem.at[u])

    ctx_load = pltpu.make_async_copy(ctx_hbm, ctx, load_sem.at[8])
    cot_load(0).start()
    ctx_load.start()
    for u in range(1, 8):
        cot_load(u).start()

    def unit(u):
        cot_load(u).wait()

        @pl.loop(0, 4)
        def _(r):
            part = pl.ds(pl.multiple_of(r * (tok // 4), tok // 4), tok // 4)
            cot_t[:, part] = cot[u, part, :].T

        base = pl.multiple_of(unit_cols(u), 128)
        tile = width // 6

        @pl.loop(0, 6)
        def _(i):
            cols = pl.ds(pl.multiple_of(i * tile, tile), tile)
            p[pl.ds(base, unit_rows), cols] = jnp.dot(
                cot_t[...], ctx[:, cols], preferred_element_type=F32).astype(BF16)

    side = (pl.ds(0, half), pl.ds(half, half))

    def rows_of(j, s):
        return pl.ds(pl.multiple_of(j * rack_rows + target(s) * step_rows, 16), step_rows)

    def message(kind, s):
        j, h, to = (
            (opp, 0, left), (right, 0, right), (opp, 1, right), (left, 1, left),
            (left, 0, left), (right, 1, right))[kind]
        return pltpu.make_async_remote_copy(
            src_ref=p.at[rows_of(j, s), side[h]],
            dst_ref=xr.at[s, kind],
            send_sem=xs_sem.at[s, kind],
            recv_sem=xr_sem.at[s, kind],
            device_id={"rack": to}, device_id_type=MESH)

    def add_into(rows, h, received):
        @pl.loop(0, step_rows // 16)
        def _(r):
            here = pl.ds(pl.multiple_of(rows.start + r * 16, 16), 16)
            there = pl.ds(pl.multiple_of(r * 16, 16), 16)
            total = p[here, side[h]].astype(F32)
            for s, kind in received:
                total = total + xr[s, kind, there, :].astype(F32)
            p[here, side[h]] = total.astype(BF16)

    def first_hops(s):
        for kind in (0, 2, 3, 1):
            message(kind, s).start()

    def relay(s):
        message(0, s).wait_recv()
        add_into(rows_of(left, s), 0, ((s, 0),))
        message(4, s).start()
        message(2, s).wait_recv()
        add_into(rows_of(right, s), 1, ((s, 2),))
        message(5, s).start()

    def block_send(s, c):
        to = target(s) * 2 + c
        start = k * rack_rows + target(s) * step_rows + c * rows48
        return pltpu.make_async_remote_copy(
            src_ref=p.at[pl.ds(pl.multiple_of(start, 16), rows48)],
            dst_ref=blocks.at[o],
            send_sem=as_sem.at[s, c],
            recv_sem=ar_sem.at[o],
            device_id={"outer": to}, device_id_type=MESH)

    def block_recv(q):
        return pltpu.make_async_remote_copy(
            src_ref=blocks.at[q], dst_ref=blocks.at[q], send_sem=as_sem.at[0, 0],
            recv_sem=ar_sem.at[q], device_id={"outer": q}, device_id_type=MESH)

    def peer_send():
        to = o ^ 1
        start = k * rack_rows + to * rows48
        return pltpu.make_async_remote_copy(
            src_ref=p.at[pl.ds(pl.multiple_of(start, 16), rows48)],
            dst_ref=blocks.at[o],
            send_sem=as_sem.at[7, 0],
            recv_sem=ar_sem.at[o],
            device_id={"outer": to}, device_id_type=MESH)

    def finish(s):
        rows = rows_of(k, s)
        message(1, s).wait_recv()
        message(4, s).wait_recv()
        add_into(rows, 0, ((s, 1), (s, 4)))
        message(3, s).wait_recv()
        message(5, s).wait_recv()
        add_into(rows, 1, ((s, 3), (s, 5)))
        if s < 7:
            for c in range(2):
                block_send(s, c).start()
        else:
            peer_send().start()
            start = k * rack_rows + o * rows48
            blocks[o] = p[pl.ds(pl.multiple_of(start, 16), rows48), :]

    def gram(s):
        q0 = source(s) * 2
        if s < 7:
            block_recv(q0).wait_recv()
            block_recv(q0 + 1).wait_recv()
        else:
            block_recv(o ^ 1).wait_recv()

        def older(m, carry):
            q = source(m // 2) * 2 + m % 2
            sums = [jnp.zeros((8, 128), F32), jnp.zeros((8, 128), F32)]
            for r in range(rows48 // 16):
                rows = pl.ds(r * 16, 16)
                for c in range(width // 128):
                    cols = pl.ds(c * 128, 128)
                    other = blocks[q, rows, cols].astype(F32)
                    for i in range(2):
                        product = blocks[q0 + i, rows, cols].astype(F32) * other
                        sums[i] = sums[i] + product[0:8] + product[8:16]
            for i in range(2):
                line = jnp.sum(sums[i], axis=0, keepdims=True)
                pairs[q0 + i, pl.ds(q, 1), :] = line
                pairs[q, pl.ds(q0 + i, 1), :] = line
            return carry

        lax.fori_loop(0, 2 * s + 2, older, 0)

    ctx_load.wait()
    unit(0)
    pl.semaphore_wait(barrier, n_rack * n_tp - 1 + n_outer - 1)
    for s in range(2):
        for kind in (0, 2):
            message(kind, s).start()
    unit(1)
    unit(2)
    for s in range(2):
        for kind in (3, 1):
            message(kind, s).start()
    unit(3)
    for s in range(8):
        relay(s)
        if s + 2 < 8:
            if s == 2:
                unit(5)
                unit(6)
            if s < 2:
                first_hops(s + 2)
                if s == 1:
                    unit(4)
            else:
                first_hops(s + 2)
        if s == 3:
            unit(7)
        if s >= 1:
            finish(s - 1)
        if s >= 4:
            gram(s - 4)
    for s in range(4, 7):
        gram(s)
    finish(7)
    gram(7)

    rowsum = jnp.sum(pairs[...], axis=2, keepdims=True)
    j_index = lax.broadcasted_iota(jnp.int32, (n_outer, n_outer, 128), 1)
    lanes = lax.broadcasted_iota(jnp.int32, (n_outer, n_outer, 128), 2)
    me1 = k * n_tp + t
    g1[me1] = jnp.sum(jnp.where(j_index == lanes, rowsum, 0.0), axis=1)

    def share1(d):
        to_k, to_t = (k + d // n_tp) % n_rack, (t + d % n_tp) % n_tp
        return pltpu.make_async_remote_copy(
            src_ref=g1.at[me1], dst_ref=g1.at[me1], send_sem=gs_sem.at[0, d],
            recv_sem=gr_sem.at[0, me1], device_id={"rack": to_k, "tp": to_t}, device_id_type=MESH)

    def share1_recv(d):
        from_k, from_t = (k + d // n_tp) % n_rack, (t + d % n_tp) % n_tp
        q = from_k * n_tp + from_t
        return pltpu.make_async_remote_copy(
            src_ref=g1.at[q], dst_ref=g1.at[q], send_sem=gs_sem.at[0, d],
            recv_sem=gr_sem.at[0, q], device_id={"rack": from_k, "tp": from_t}, device_id_type=MESH)

    for d in range(1, n_rack * n_tp):
        share1(d).start()
    for d in range(1, n_rack * n_tp):
        share1_recv(d).wait_recv()
    g2[o] = jnp.sum(g1[...], axis=0)

    def share2(d):
        return pltpu.make_async_remote_copy(
            src_ref=g2.at[o], dst_ref=g2.at[o], send_sem=gs_sem.at[1, d],
            recv_sem=gr_sem.at[1, o], device_id={"outer": (o + d) % n_outer}, device_id_type=MESH)

    def share2_recv(d):
        q = (o + d) % n_outer
        return pltpu.make_async_remote_copy(
            src_ref=g2.at[q], dst_ref=g2.at[q], send_sem=gs_sem.at[1, d],
            recv_sem=gr_sem.at[1, q], device_id={"outer": q}, device_id_type=MESH)

    for d in range(1, n_outer):
        share2(d).start()
    for d in range(1, n_outer):
        share2_recv(d).wait_recv()
    weights = merge_weights(jnp.sum(g2[...], axis=0), n_outer, 4)

    spread = [jnp.broadcast_to(weights[q:q + 1, 0:1], (16, 128)) for q in range(n_outer)]
    for r in range(rows48 // 16):
        for c in range(width // 128):
            at = (pl.ds(r * 16, 16), pl.ds(c * 128, 128))
            total = spread[0] * blocks[(0,) + at].astype(F32)
            for q in range(1, n_outer):
                total = total + spread[q] * blocks[(q,) + at].astype(F32)
            out_ref[at] = total.astype(BF16)

    for s in range(8):
        for kind in range(6):
            message(kind, s).wait_send()
        if s < 7:
            for c in range(2):
                block_send(s, c).wait_send()
    peer_send().wait_send()
    for d in range(1, n_rack * n_tp):
        share1(d).wait_send()
    for d in range(1, n_outer):
        share2(d).wait_send()


def shards(context, cotangent):
    tok, width = context.shape
    cols = cotangent.shape[1]
    n_outer = lax.axis_size("outer")
    rack_rows = cols // 4
    rows48 = rack_rows // 16
    return pl.pallas_call(
        kernel,
        out_shape=jax.ShapeDtypeStruct((rows48, width), BF16),
        in_specs=[pl.BlockSpec(memory_space=pl.ANY)] * 2,
        out_specs=pl.BlockSpec(memory_space=pltpu.VMEM),
        scratch_shapes=[
            pltpu.VMEM((tok, width), BF16),
            pltpu.VMEM((8, tok, rack_rows // 2), BF16),
            pltpu.VMEM((rack_rows // 2, tok), BF16),
            pltpu.VMEM((cols, width), BF16),
            pltpu.VMEM((8, 6, 2 * rows48, width // 2), BF16),
            pltpu.VMEM((n_outer, rows48, width), BF16),
            pltpu.VMEM((n_outer, n_outer, 128), F32),
            pltpu.VMEM((16, n_outer, 128), F32),
            pltpu.VMEM((16, n_outer, 128), F32),
            pltpu.SemaphoreType.DMA((9,)),
            pltpu.SemaphoreType.DMA((8, 6)),
            pltpu.SemaphoreType.DMA((8, 6)),
            pltpu.SemaphoreType.DMA((8, 2)),
            pltpu.SemaphoreType.DMA((16,)),
            pltpu.SemaphoreType.DMA((2, 16)),
            pltpu.SemaphoreType.DMA((2, 16)),
        ],
        compiler_params=pltpu.CompilerParams(
            collective_id=0, has_side_effects=True, vmem_limit_bytes=56 * 2**20),
    )(context, cotangent)


def solution(mesh):
    return jax.shard_map(
        shards,
        mesh=mesh,
        in_specs=(P(("rack", "outer"), "tp"), P(("rack", "outer"), None)),
        out_specs=P(("rack", "outer"), "tp"),
        check_vma=False,
    )
```

```python
import functools
import jax
import jax.numpy as jnp
from jax import lax
from jax.experimental import pallas as pl
from jax.experimental.pallas import tpu as pltpu
from jax.sharding import PartitionSpec as P

EPS = 1e-06
MESH = pl.DeviceIdType.MESH
F32 = jnp.float32
BF16 = jnp.bfloat16


def xor_roll(x, distance, axis, index, size):
    up = pltpu.roll(x, x.shape[axis] - distance, axis)
    down = pltpu.roll(x, distance, axis)
    return jnp.where((index & distance) == 0, up, down)


def merge_weights(gram, n, levels):
    row = lax.broadcasted_iota(jnp.int32, gram.shape, 0)
    lane = lax.broadcasted_iota(jnp.int32, gram.shape, 1)
    diagonal = row == lane
    weights_t = jnp.where(diagonal, 1.0, 0.0).astype(F32)

    def mixing(aa, bb, ab):
        aa, bb = jnp.maximum(aa, 0.0), jnp.maximum(bb, 0.0)
        bound = jnp.sqrt(aa) * jnp.sqrt(bb)
        ab = jnp.clip(ab, -bound, bound)
        return 1.0 - ab / (2.0 * (aa + EPS)), 1.0 - ab / (2.0 * (bb + EPS))

    for level in range(levels):
        d = 1 << level
        partner = (row ^ d) == lane
        gram_r = xor_roll(gram, d, 0, row, n)
        gram_l = xor_roll(gram, d, 1, lane, n)

        def column(x, mask):
            return jnp.sum(jnp.where(mask, x, 0.0), axis=1, keepdims=True)

        def line(x, mask):
            return jnp.sum(jnp.where(mask, x, 0.0), axis=0, keepdims=True)

        ca, cb = mixing(column(gram, diagonal), column(gram_r, partner), column(gram, partner))
        ra, rb = mixing(line(gram, diagonal), line(gram_l, partner), line(gram, partner))
        mixed = ca * gram + cb * gram_r
        gram = ra * mixed + rb * xor_roll(mixed, d, 1, lane, n)
        weights_t = ra * weights_t + rb * xor_roll(weights_t, d, 1, lane, n)
    return weights_t[:, 0:1]


def kernel(ctx_hbm, cot_hbm, out_ref, ctx, cot, p, xr, blocks, pairs, g1, g2,
           load_sem, xs_sem, xr_sem, as_sem, ar_sem, gs_sem, gr_sem, near_sem, far_sem, core_sem):
    n_rack, n_outer, n_tp = lax.axis_size("rack"), lax.axis_size("outer"), lax.axis_size("tp")
    k, o, t = lax.axis_index("rack"), lax.axis_index("outer"), lax.axis_index("tp")
    left, right, opp = (k + 3) % 4, (k + 1) % 4, (k + 2) % 4
    z, core = o // 2, o % 2
    zh, zl = z // 4, z % 4
    tok, width = ctx.shape
    half = width // 2
    rack_rows = p.shape[0] // 4
    rows48 = rack_rows // 16
    step_rows = 2 * rows48
    unit_rows = rack_rows // 2
    dest = (opp, right, left, k)

    def along_z(d):
        return {"outer": (z + d) % 8 * 2 + core}

    adjacent = [{"rack": left}, {"rack": right}, {"tp": (t + 1) % 4}, {"tp": (t + 3) % 4},
                along_z(1), along_z(7)]
    second = [{"rack": left}, {"rack": right}, {"rack": opp}, along_z(2), along_z(6)]
    barrier = pltpu.get_barrier_semaphore()
    for device in adjacent + [{"outer": o ^ 1}]:
        pl.semaphore_signal(barrier, inc=1, device_id=device, device_id_type=MESH)

    def greet(semaphore, devices):
        for device in devices:
            pl.semaphore_signal(semaphore, inc=1, device_id=device, device_id_type=MESH)

    def target(s):
        h = s // 4
        return (zh ^ (1 - h)) * 4 + (zl ^ (s + h * (7 - 2 * s)))

    def unit_cols(u):
        h = zh ^ (1 - u // 4)
        return dest[u % 4] * rack_rows + h * unit_rows

    def cot_load(u):
        cols = pl.ds(pl.multiple_of(unit_cols(u), 128), unit_rows)
        return pltpu.make_async_copy(cot_hbm.at[:, cols], cot.at[u], load_sem.at[u])

    def ctx_load(h):
        cols = pl.ds(h * half, half)
        return pltpu.make_async_copy(ctx_hbm.at[:, cols], ctx.at[:, cols], load_sem.at[8 + h])

    cot_load(0).start()
    for h in range(2):
        ctx_load(h).start()
    for u in range(1, 8):
        cot_load(u).start()

    def product(u, h):
        cols = pl.ds(pl.multiple_of(h * half, half), half)
        p[pl.ds(pl.multiple_of(unit_cols(u), 128), unit_rows), cols] = lax.dot_general(
            cot[u], ctx[:, cols], (((0,), (0,)), ((), ())),
            preferred_element_type=F32).astype(BF16)

    def unit(u):
        cot_load(u).wait()

        @pl.loop(0, 2)
        def _(h):
            product(u, h)

    part = half // 3
    pieces = [(s, 0, half) for s in range(7)] + [(7, i * part, part) for i in range(3)]

    def side(h, i):
        _, first, size = pieces[i]
        return pl.ds(h * half + first, size)

    def rows_of(j, s):
        return pl.ds(pl.multiple_of(j * rack_rows + target(s) * step_rows, 16), step_rows)

    def message(kind, i):
        s, first, size = pieces[i]
        j, h, to = (
            (opp, 0, left), (right, 0, right), (opp, 1, right), (left, 1, left),
            (left, 0, left), (right, 1, right))[kind]
        return pltpu.make_async_remote_copy(
            src_ref=p.at[rows_of(j, s), side(h, i)],
            dst_ref=xr.at[s, kind, :, pl.ds(first, size)],
            send_sem=xs_sem.at[i, kind],
            recv_sem=xr_sem.at[i, kind],
            device_id={"rack": to}, device_id_type=MESH)

    def add_into(j, h, i, kinds):
        s, first, size = pieces[i]
        rows = rows_of(j, s)

        @pl.loop(0, step_rows // 16)
        def _(r):
            here = pl.ds(pl.multiple_of(rows.start + r * 16, 16), 16)
            there = pl.ds(pl.multiple_of(r * 16, 16), 16)
            total = p[here, side(h, i)].astype(F32)
            for kind in kinds:
                total = total + xr[s, kind, there, pl.ds(first, size)].astype(F32)
            p[here, side(h, i)] = total.astype(BF16)

    def first_hops(i):
        for kind in (0, 2, 3, 1):
            message(kind, i).start()

    def relay(i):
        message(0, i).wait_recv()
        add_into(left, 0, i, (0,))
        message(4, i).start()
        message(2, i).wait_recv()
        add_into(right, 1, i, (2,))
        message(5, i).start()

    def block_send(s, c):
        to = target(s) * 2 + c
        start = k * rack_rows + target(s) * step_rows + c * rows48
        return pltpu.make_async_remote_copy(
            src_ref=p.at[pl.ds(pl.multiple_of(start, 16), rows48)],
            dst_ref=blocks.at[o],
            send_sem=as_sem.at[s, c],
            recv_sem=ar_sem.at[o],
            device_id={"outer": to}, device_id_type=MESH)

    def block_recv(q):
        return pltpu.make_async_remote_copy(
            src_ref=blocks.at[q], dst_ref=blocks.at[q], send_sem=as_sem.at[0, 0],
            recv_sem=ar_sem.at[q], device_id={"outer": q}, device_id_type=MESH)

    def peer_copy(h, i, slot):
        start = k * rack_rows + (o ^ 1) * rows48
        return pltpu.make_async_remote_copy(
            src_ref=p.at[pl.ds(pl.multiple_of(start, 16), rows48), side(h, i)],
            dst_ref=blocks.at[slot, :, side(h, i)],
            send_sem=as_sem.at[i, h],
            recv_sem=ar_sem.at[n_outer + 2 * (i - 7) + h],
            device_id={"outer": o ^ 1}, device_id_type=MESH)

    def finish(i):
        s = pieces[i][0]
        for h, kinds in ((0, (1, 4)), (1, (3, 5))):
            for kind in kinds:
                message(kind, i).wait_recv()
            add_into(k, h, i, kinds)
            if s == 7:
                peer_copy(h, i, o).start()
        if s < 7:
            for c in range(2):
                block_send(s, c).start()
        else:
            start = pl.multiple_of(k * rack_rows + o * rows48, 16)
            for h in range(2):
                blocks[o, :, side(h, i)] = p[pl.ds(start, rows48), side(h, i)]

    def gram(i):
        s, first, size = pieces[i]
        q0 = target(s) * 2
        if s < 7:
            block_recv(q0).wait_recv()
            block_recv(q0 + 1).wait_recv()
        else:
            for h in range(2):
                peer_copy(h, i, o ^ 1).wait_recv()

        def inner(q, newer):
            sums = [jnp.zeros((8, 128), F32) for _ in newer]
            for r in range(rows48 // 16):
                rows = pl.ds(r * 16, 16)
                for c in range(2 * size // 128):
                    h, c = c // (size // 128), c % (size // 128)
                    cols = pl.ds(h * half + first + c * 128, 128)
                    other = blocks[q, rows, cols].astype(F32)
                    for n, a in enumerate(newer):
                        term = blocks[q0 + a, rows, cols].astype(F32) * other
                        sums[n] = sums[n] + term[0:8] + term[8:16]
            for n, a in enumerate(newer):
                line = jnp.sum(sums[n], axis=0, keepdims=True)
                if first > 0:
                    line = line + pairs[q0 + a, pl.ds(q, 1), :]
                pairs[q0 + a, pl.ds(q, 1), :] = line
                pairs[q, pl.ds(q0 + a, 1), :] = line

        @pl.loop(0, 2 * s + 1)
        def _(m):
            inner(target(m // 2) * 2 + m % 2, (0, 1))

        inner(q0 + 1, (1,))

    cot_load(0).wait()
    ctx_load(0).wait()
    product(0, 0)
    pl.semaphore_wait(barrier, 7)
    message(0, 0).start()
    message(0, 1).start()
    greet(near_sem, adjacent)
    ctx_load(1).wait()
    product(0, 1)
    message(2, 0).start()
    message(2, 1).start()
    unit(2)
    message(3, 0).start()
    unit(1)
    message(1, 0).start()
    pl.semaphore_wait(near_sem, 6)
    greet(far_sem, second)
    message(3, 1).start()
    message(1, 1).start()
    unit(3)
    pl.semaphore_wait(far_sem, 5)
    greet(core_sem, [{"outer": o ^ 1}])
    for s in range(7):
        relay(s)
        if s == 0:
            pl.semaphore_wait(core_sem, 1)
        if s + 2 < 7:
            if s == 2:
                unit(6)
                unit(5)
            first_hops(s + 2)
        if s == 6:
            for kinds in ((0, 2), (3, 1)):
                for i in (7, 8, 9):
                    for kind in kinds:
                        message(kind, i).start()
        if s == 1:
            unit(4)
        if s == 3:
            unit(7)
        if s >= 1:
            finish(s - 1)
        if s >= 3:
            gram(s - 3)
    finish(6)
    for i in (7, 8, 9):
        relay(i)
    gram(4)
    gram(5)
    finish(7)
    gram(6)
    finish(8)
    gram(7)
    finish(9)
    gram(8)
    gram(9)

    rowsum = jnp.sum(pairs[...], axis=2, keepdims=True)
    j_index = lax.broadcasted_iota(jnp.int32, (n_outer, n_outer, 128), 1)
    lanes = lax.broadcasted_iota(jnp.int32, (n_outer, n_outer, 128), 2)
    me1 = k * n_tp + t
    g1[me1] = jnp.sum(jnp.where(j_index == lanes, rowsum, 0.0), axis=1)

    def share1(d):
        to_k, to_t = (k + d // n_tp) % n_rack, (t + d % n_tp) % n_tp
        return pltpu.make_async_remote_copy(
            src_ref=g1.at[me1], dst_ref=g1.at[me1], send_sem=gs_sem.at[0, d],
            recv_sem=gr_sem.at[0, me1], device_id={"rack": to_k, "tp": to_t}, device_id_type=MESH)

    def share1_recv(d):
        from_k, from_t = (k + d // n_tp) % n_rack, (t + d % n_tp) % n_tp
        q = from_k * n_tp + from_t
        return pltpu.make_async_remote_copy(
            src_ref=g1.at[q], dst_ref=g1.at[q], send_sem=gs_sem.at[0, d],
            recv_sem=gr_sem.at[0, q], device_id={"rack": from_k, "tp": from_t}, device_id_type=MESH)

    for d in range(1, n_rack * n_tp):
        share1(d).start()
    for i in range(10):
        for kind in range(6):
            message(kind, i).wait_send()
        for h in range(2):
            if i < 7:
                block_send(i, h).wait_send()
            else:
                peer_copy(h, i, o).wait_send()
    for d in range(1, n_rack * n_tp):
        share1_recv(d).wait_recv()
    g2[o] = jnp.sum(g1[...], axis=0)

    def share2(d):
        return pltpu.make_async_remote_copy(
            src_ref=g2.at[o], dst_ref=g2.at[o], send_sem=gs_sem.at[1, d],
            recv_sem=gr_sem.at[1, o], device_id={"outer": (o + d) % n_outer}, device_id_type=MESH)

    def share2_recv(d):
        q = (o + d) % n_outer
        return pltpu.make_async_remote_copy(
            src_ref=g2.at[q], dst_ref=g2.at[q], send_sem=gs_sem.at[1, d],
            recv_sem=gr_sem.at[1, q], device_id={"outer": q}, device_id_type=MESH)

    for d in range(1, n_outer):
        share2(d).start()
    for d in range(1, n_outer):
        share2_recv(d).wait_recv()
    weights = merge_weights(jnp.sum(g2[...], axis=0), n_outer, 4)

    spread = [jnp.broadcast_to(weights[q:q + 1, 0:1], (16, 128)) for q in range(n_outer)]
    for r in range(rows48 // 16):
        for c in range(width // 128):
            at = (pl.ds(r * 16, 16), pl.ds(c * 128, 128))
            total = spread[0] * blocks[(0,) + at].astype(F32)
            for q in range(1, n_outer):
                total = total + spread[q] * blocks[(q,) + at].astype(F32)
            out_ref[at] = total.astype(BF16)

    for d in range(1, n_rack * n_tp):
        share1(d).wait_send()
    for d in range(1, n_outer):
        share2(d).wait_send()


def shards(context, cotangent):
    tok, width = context.shape
    cols = cotangent.shape[1]
    n_outer = lax.axis_size("outer")
    rack_rows = cols // 4
    rows48 = rack_rows // 16
    return pl.pallas_call(
        kernel,
        out_shape=jax.ShapeDtypeStruct((rows48, width), BF16),
        in_specs=[pl.BlockSpec(memory_space=pl.ANY)] * 2,
        out_specs=pl.BlockSpec(memory_space=pltpu.VMEM),
        scratch_shapes=[
            pltpu.VMEM((tok, width), BF16),
            pltpu.VMEM((8, tok, rack_rows // 2), BF16),
            pltpu.VMEM((cols, width), BF16),
            pltpu.VMEM((8, 6, 2 * rows48, width // 2), BF16),
            pltpu.VMEM((n_outer, rows48, width), BF16),
            pltpu.VMEM((n_outer, n_outer, 128), F32),
            pltpu.VMEM((16, n_outer, 128), F32),
            pltpu.VMEM((16, n_outer, 128), F32),
            pltpu.SemaphoreType.DMA((10,)),
            pltpu.SemaphoreType.DMA((10, 6)),
            pltpu.SemaphoreType.DMA((10, 6)),
            pltpu.SemaphoreType.DMA((10, 2)),
            pltpu.SemaphoreType.DMA((22,)),
            pltpu.SemaphoreType.DMA((2, 16)),
            pltpu.SemaphoreType.DMA((2, 16)),
            pltpu.SemaphoreType.REGULAR,
            pltpu.SemaphoreType.REGULAR,
            pltpu.SemaphoreType.REGULAR,
        ],
        compiler_params=pltpu.CompilerParams(
            collective_id=0, has_side_effects=True, vmem_limit_bytes=56 * 2**20),
    )(context, cotangent)


def solution(mesh):
    return jax.shard_map(
        shards,
        mesh=mesh,
        in_specs=(P(("rack", "outer"), "tp"), P(("rack", "outer"), None)),
        out_specs=P(("rack", "outer"), "tp"),
        check_vma=False,
    )
```

```python
import functools
import jax
import jax.numpy as jnp
from jax import lax
from jax.experimental import pallas as pl
from jax.experimental.pallas import tpu as pltpu
from jax.sharding import PartitionSpec as P

EPS = 1e-06
MESH = pl.DeviceIdType.MESH
F32 = jnp.float32
BF16 = jnp.bfloat16


def xor_roll(x, distance, axis, index, size):
    up = pltpu.roll(x, x.shape[axis] - distance, axis)
    down = pltpu.roll(x, distance, axis)
    return jnp.where((index & distance) == 0, up, down)


def merge_weights(gram, n, levels):
    row = lax.broadcasted_iota(jnp.int32, gram.shape, 0)
    lane = lax.broadcasted_iota(jnp.int32, gram.shape, 1)
    diagonal = row == lane
    weights_t = jnp.where(diagonal, 1.0, 0.0).astype(F32)

    def mixing(aa, bb, ab):
        aa, bb = jnp.maximum(aa, 0.0), jnp.maximum(bb, 0.0)
        bound = jnp.sqrt(aa) * jnp.sqrt(bb)
        ab = jnp.clip(ab, -bound, bound)
        return 1.0 - ab / (2.0 * (aa + EPS)), 1.0 - ab / (2.0 * (bb + EPS))

    for level in range(levels):
        d = 1 << level
        partner = (row ^ d) == lane
        gram_r = xor_roll(gram, d, 0, row, n)
        gram_l = xor_roll(gram, d, 1, lane, n)

        def column(x, mask):
            return jnp.sum(jnp.where(mask, x, 0.0), axis=1, keepdims=True)

        def line(x, mask):
            return jnp.sum(jnp.where(mask, x, 0.0), axis=0, keepdims=True)

        ca, cb = mixing(column(gram, diagonal), column(gram_r, partner), column(gram, partner))
        ra, rb = mixing(line(gram, diagonal), line(gram_l, partner), line(gram, partner))
        mixed = ca * gram + cb * gram_r
        gram = ra * mixed + rb * xor_roll(mixed, d, 1, lane, n)
        weights_t = ra * weights_t + rb * xor_roll(weights_t, d, 1, lane, n)
    return weights_t[:, 0:1]


def kernel(ctx_hbm, cot_hbm, out_ref, ctx, cot, p, xr, blocks, pairs, g1, g2,
           load_sem, xs_sem, xr_sem, as_sem, ar_sem, gs_sem, gr_sem, near_sem, far_sem, core_sem):
    n_rack, n_outer, n_tp = lax.axis_size("rack"), lax.axis_size("outer"), lax.axis_size("tp")
    k, o, t = lax.axis_index("rack"), lax.axis_index("outer"), lax.axis_index("tp")
    left, right, opp = (k + 3) % 4, (k + 1) % 4, (k + 2) % 4
    z, core = o // 2, o % 2
    zh, zl = z // 4, z % 4
    tok, width = ctx.shape
    half = width // 2
    rack_rows = p.shape[0] // 4
    rows48 = rack_rows // 16
    step_rows = 2 * rows48
    unit_rows = rack_rows // 2
    dest = (opp, right, left, k)

    def along_z(d):
        return {"outer": (z + d) % 8 * 2 + core}

    adjacent = [{"rack": left}, {"rack": right}, {"tp": (t + 1) % 4}, {"tp": (t + 3) % 4},
                along_z(1), along_z(7)]
    second = [{"rack": left}, {"rack": right}, {"rack": opp}, along_z(2), along_z(6)]
    barrier = pltpu.get_barrier_semaphore()
    for device in adjacent + [{"outer": o ^ 1}]:
        pl.semaphore_signal(barrier, inc=1, device_id=device, device_id_type=MESH)

    def greet(semaphore, devices):
        for device in devices:
            pl.semaphore_signal(semaphore, inc=1, device_id=device, device_id_type=MESH)

    def distance(s):
        odd = s % 2
        return (1 - odd) * (4 + s // 2) + odd * ((7 - s) // 2)

    def target(s):
        return (z + distance(s)) % 8

    def source(s):
        return (z + 8 - distance(s)) % 8

    def unit_cols(u):
        h = zh ^ (1 - u // 4)
        return dest[u % 4] * rack_rows + h * unit_rows

    def cot_load(u):
        cols = pl.ds(pl.multiple_of(unit_cols(u), 128), unit_rows)
        return pltpu.make_async_copy(cot_hbm.at[:, cols], cot.at[u], load_sem.at[u])

    def ctx_load(h):
        cols = pl.ds(h * half, half)
        return pltpu.make_async_copy(ctx_hbm.at[:, cols], ctx.at[:, cols], load_sem.at[8 + h])

    cot_load(0).start()
    for h in range(2):
        ctx_load(h).start()
    for u in range(1, 8):
        cot_load(u).start()

    def product(u, h):
        cols = pl.ds(pl.multiple_of(h * half, half), half)
        p[pl.ds(pl.multiple_of(unit_cols(u), 128), unit_rows), cols] = lax.dot_general(
            cot[u], ctx[:, cols], (((0,), (0,)), ((), ())),
            preferred_element_type=F32).astype(BF16)

    def unit(u):
        cot_load(u).wait()

        @pl.loop(0, 2)
        def _(h):
            product(u, h)

    part = half // 3
    pieces = [(s, 0, half) for s in range(7)] + [(7, i * part, part) for i in range(3)]

    def side(h, i):
        _, first, size = pieces[i]
        return pl.ds(h * half + first, size)

    def rows_of(j, s):
        return pl.ds(pl.multiple_of(j * rack_rows + target(s) * step_rows, 16), step_rows)

    def message(kind, i):
        s, first, size = pieces[i]
        j, h, to = (
            (opp, 0, left), (right, 0, right), (opp, 1, right), (left, 1, left),
            (left, 0, left), (right, 1, right))[kind]
        return pltpu.make_async_remote_copy(
            src_ref=p.at[rows_of(j, s), side(h, i)],
            dst_ref=xr.at[s, kind, :, pl.ds(first, size)],
            send_sem=xs_sem.at[i, kind],
            recv_sem=xr_sem.at[i, kind],
            device_id={"rack": to}, device_id_type=MESH)

    def add_into(j, h, i, kinds):
        s, first, size = pieces[i]
        rows = rows_of(j, s)

        @pl.loop(0, step_rows // 16)
        def _(r):
            here = pl.ds(pl.multiple_of(rows.start + r * 16, 16), 16)
            there = pl.ds(pl.multiple_of(r * 16, 16), 16)
            total = p[here, side(h, i)].astype(F32)
            for kind in kinds:
                total = total + xr[s, kind, there, pl.ds(first, size)].astype(F32)
            p[here, side(h, i)] = total.astype(BF16)

    def first_hops(i):
        for kind in (0, 2, 3, 1):
            message(kind, i).start()

    def relay(i):
        message(0, i).wait_recv()
        add_into(left, 0, i, (0,))
        message(4, i).start()
        message(2, i).wait_recv()
        add_into(right, 1, i, (2,))
        message(5, i).start()

    def block_send(s, c):
        to = target(s) * 2 + c
        start = k * rack_rows + target(s) * step_rows + c * rows48
        return pltpu.make_async_remote_copy(
            src_ref=p.at[pl.ds(pl.multiple_of(start, 16), rows48)],
            dst_ref=blocks.at[o],
            send_sem=as_sem.at[s, c],
            recv_sem=ar_sem.at[o],
            device_id={"outer": to}, device_id_type=MESH)

    def block_recv(q):
        return pltpu.make_async_remote_copy(
            src_ref=blocks.at[q], dst_ref=blocks.at[q], send_sem=as_sem.at[0, 0],
            recv_sem=ar_sem.at[q], device_id={"outer": q}, device_id_type=MESH)

    def peer_copy(h, i, slot):
        start = k * rack_rows + (o ^ 1) * rows48
        return pltpu.make_async_remote_copy(
            src_ref=p.at[pl.ds(pl.multiple_of(start, 16), rows48), side(h, i)],
            dst_ref=blocks.at[slot, :, side(h, i)],
            send_sem=as_sem.at[i, h],
            recv_sem=ar_sem.at[n_outer + 2 * (i - 7) + h],
            device_id={"outer": o ^ 1}, device_id_type=MESH)

    def finish(i):
        s = pieces[i][0]
        for h, kinds in ((0, (1, 4)), (1, (3, 5))):
            for kind in kinds:
                message(kind, i).wait_recv()
            add_into(k, h, i, kinds)
            if s == 7:
                peer_copy(h, i, o).start()
        if s < 7:
            for c in range(2):
                block_send(s, c).start()
        else:
            start = pl.multiple_of(k * rack_rows + o * rows48, 16)
            for h in range(2):
                blocks[o, :, side(h, i)] = p[pl.ds(start, rows48), side(h, i)]

    def gram(i):
        s, first, size = pieces[i]
        q0 = source(s) * 2
        if s < 7:
            block_recv(q0).wait_recv()
            block_recv(q0 + 1).wait_recv()
        else:
            for h in range(2):
                peer_copy(h, i, o ^ 1).wait_recv()

        def inner(q, newer):
            sums = [jnp.zeros((8, 128), F32) for _ in newer]
            for r in range(rows48 // 16):
                rows = pl.ds(r * 16, 16)
                for c in range(2 * size // 128):
                    h, c = c // (size // 128), c % (size // 128)
                    cols = pl.ds(h * half + first + c * 128, 128)
                    other = blocks[q, rows, cols].astype(F32)
                    for n, a in enumerate(newer):
                        term = blocks[q0 + a, rows, cols].astype(F32) * other
                        sums[n] = sums[n] + term[0:8] + term[8:16]
            for n, a in enumerate(newer):
                line = jnp.sum(sums[n], axis=0, keepdims=True)
                if first > 0:
                    line = line + pairs[q0 + a, pl.ds(q, 1), :]
                pairs[q0 + a, pl.ds(q, 1), :] = line
                pairs[q, pl.ds(q0 + a, 1), :] = line

        @pl.loop(0, 2 * s + 1)
        def _(m):
            inner(source(m // 2) * 2 + m % 2, (0, 1))

        inner(q0 + 1, (1,))

    cot_load(0).wait()
    ctx_load(0).wait()
    product(0, 0)
    pl.semaphore_wait(barrier, 7)
    message(0, 0).start()
    greet(near_sem, adjacent)
    ctx_load(1).wait()
    product(0, 1)
    message(2, 0).start()
    unit(2)
    message(3, 0).start()
    unit(1)
    message(1, 0).start()
    pl.semaphore_wait(near_sem, 6)
    greet(far_sem, second)
    unit(4)
    message(0, 1).start()
    message(2, 1).start()
    relay(0)
    unit(6)
    message(3, 1).start()
    unit(5)
    message(1, 1).start()
    pl.semaphore_wait(far_sem, 5)
    greet(core_sem, [{"outer": o ^ 1}])
    first_hops(2)
    unit(3)
    unit(7)
    pl.semaphore_wait(core_sem, 1)
    for s in range(1, 7):
        relay(s)
        if s + 2 < 7:
            first_hops(s + 2)
        if s == 6:
            for kinds in ((0, 2), (3, 1)):
                for i in (7, 8, 9):
                    for kind in kinds:
                        message(kind, i).start()
        finish(s - 1)
        if s >= 3:
            gram(s - 3)
    finish(6)
    for i in (7, 8, 9):
        relay(i)
    gram(4)
    gram(5)
    finish(7)
    gram(6)
    finish(8)
    gram(7)
    finish(9)
    gram(8)
    gram(9)

    rowsum = jnp.sum(pairs[...], axis=2, keepdims=True)
    j_index = lax.broadcasted_iota(jnp.int32, (n_outer, n_outer, 128), 1)
    lanes = lax.broadcasted_iota(jnp.int32, (n_outer, n_outer, 128), 2)
    me1 = k * n_tp + t
    g1[me1] = jnp.sum(jnp.where(j_index == lanes, rowsum, 0.0), axis=1)

    def share1(d):
        to_k, to_t = (k + d // n_tp) % n_rack, (t + d % n_tp) % n_tp
        return pltpu.make_async_remote_copy(
            src_ref=g1.at[me1], dst_ref=g1.at[me1], send_sem=gs_sem.at[0, d],
            recv_sem=gr_sem.at[0, me1], device_id={"rack": to_k, "tp": to_t}, device_id_type=MESH)

    def share1_recv(d):
        from_k, from_t = (k + d // n_tp) % n_rack, (t + d % n_tp) % n_tp
        q = from_k * n_tp + from_t
        return pltpu.make_async_remote_copy(
            src_ref=g1.at[q], dst_ref=g1.at[q], send_sem=gs_sem.at[0, d],
            recv_sem=gr_sem.at[0, q], device_id={"rack": from_k, "tp": from_t}, device_id_type=MESH)

    for d in range(1, n_rack * n_tp):
        share1(d).start()
    for i in range(10):
        for kind in range(6):
            message(kind, i).wait_send()
        for h in range(2):
            if i < 7:
                block_send(i, h).wait_send()
            else:
                peer_copy(h, i, o).wait_send()
    for d in range(1, n_rack * n_tp):
        share1_recv(d).wait_recv()
    g2[o] = jnp.sum(g1[...], axis=0)

    def share2(d):
        return pltpu.make_async_remote_copy(
            src_ref=g2.at[o], dst_ref=g2.at[o], send_sem=gs_sem.at[1, d],
            recv_sem=gr_sem.at[1, o], device_id={"outer": (o + d) % n_outer}, device_id_type=MESH)

    def share2_recv(d):
        q = (o + d) % n_outer
        return pltpu.make_async_remote_copy(
            src_ref=g2.at[q], dst_ref=g2.at[q], send_sem=gs_sem.at[1, d],
            recv_sem=gr_sem.at[1, q], device_id={"outer": q}, device_id_type=MESH)

    for d in range(1, n_outer):
        share2(d).start()
    for d in range(1, n_outer):
        share2_recv(d).wait_recv()
    weights = merge_weights(jnp.sum(g2[...], axis=0), n_outer, 4)

    spread = [jnp.broadcast_to(weights[q:q + 1, 0:1], (16, 128)) for q in range(n_outer)]
    for r in range(rows48 // 16):
        for c in range(width // 128):
            at = (pl.ds(r * 16, 16), pl.ds(c * 128, 128))
            total = spread[0] * blocks[(0,) + at].astype(F32)
            for q in range(1, n_outer):
                total = total + spread[q] * blocks[(q,) + at].astype(F32)
            out_ref[at] = total.astype(BF16)

    for d in range(1, n_rack * n_tp):
        share1(d).wait_send()
    for d in range(1, n_outer):
        share2(d).wait_send()


def shards(context, cotangent):
    tok, width = context.shape
    cols = cotangent.shape[1]
    n_outer = lax.axis_size("outer")
    rack_rows = cols // 4
    rows48 = rack_rows // 16
    return pl.pallas_call(
        kernel,
        out_shape=jax.ShapeDtypeStruct((rows48, width), BF16),
        in_specs=[pl.BlockSpec(memory_space=pl.ANY)] * 2,
        out_specs=pl.BlockSpec(memory_space=pltpu.VMEM),
        scratch_shapes=[
            pltpu.VMEM((tok, width), BF16),
            pltpu.VMEM((8, tok, rack_rows // 2), BF16),
            pltpu.VMEM((cols, width), BF16),
            pltpu.VMEM((8, 6, 2 * rows48, width // 2), BF16),
            pltpu.VMEM((n_outer, rows48, width), BF16),
            pltpu.VMEM((n_outer, n_outer, 128), F32),
            pltpu.VMEM((16, n_outer, 128), F32),
            pltpu.VMEM((16, n_outer, 128), F32),
            pltpu.SemaphoreType.DMA((10,)),
            pltpu.SemaphoreType.DMA((10, 6)),
            pltpu.SemaphoreType.DMA((10, 6)),
            pltpu.SemaphoreType.DMA((10, 2)),
            pltpu.SemaphoreType.DMA((22,)),
            pltpu.SemaphoreType.DMA((2, 16)),
            pltpu.SemaphoreType.DMA((2, 16)),
            pltpu.SemaphoreType.REGULAR,
            pltpu.SemaphoreType.REGULAR,
            pltpu.SemaphoreType.REGULAR,
        ],
        compiler_params=pltpu.CompilerParams(
            collective_id=0, has_side_effects=True, vmem_limit_bytes=56 * 2**20),
    )(context, cotangent)


def solution(mesh):
    return jax.shard_map(
        shards,
        mesh=mesh,
        in_specs=(P(("rack", "outer"), "tp"), P(("rack", "outer"), None)),
        out_specs=P(("rack", "outer"), "tp"),
        check_vma=False,
    )
```

```python
import functools
import jax
import jax.numpy as jnp
from jax import lax
from jax.experimental import pallas as pl
from jax.experimental.pallas import tpu as pltpu
from jax.sharding import PartitionSpec as P

EPS = 1e-06
MESH = pl.DeviceIdType.MESH
F32 = jnp.float32
BF16 = jnp.bfloat16


def xor_roll(x, distance, axis, index, size):
    up = pltpu.roll(x, x.shape[axis] - distance, axis)
    down = pltpu.roll(x, distance, axis)
    return jnp.where((index & distance) == 0, up, down)


def merge_weights(gram, n, levels):
    row = lax.broadcasted_iota(jnp.int32, gram.shape, 0)
    lane = lax.broadcasted_iota(jnp.int32, gram.shape, 1)
    diagonal = row == lane
    weights_t = jnp.where(diagonal, 1.0, 0.0).astype(F32)

    def mixing(aa, bb, ab):
        aa, bb = jnp.maximum(aa, 0.0), jnp.maximum(bb, 0.0)
        bound = jnp.sqrt(aa) * jnp.sqrt(bb)
        ab = jnp.clip(ab, -bound, bound)
        return 1.0 - ab / (2.0 * (aa + EPS)), 1.0 - ab / (2.0 * (bb + EPS))

    for level in range(levels):
        d = 1 << level
        partner = (row ^ d) == lane
        gram_r = xor_roll(gram, d, 0, row, n)
        gram_l = xor_roll(gram, d, 1, lane, n)

        def column(x, mask):
            return jnp.sum(jnp.where(mask, x, 0.0), axis=1, keepdims=True)

        def line(x, mask):
            return jnp.sum(jnp.where(mask, x, 0.0), axis=0, keepdims=True)

        ca, cb = mixing(column(gram, diagonal), column(gram_r, partner), column(gram, partner))
        ra, rb = mixing(line(gram, diagonal), line(gram_l, partner), line(gram, partner))
        mixed = ca * gram + cb * gram_r
        gram = ra * mixed + rb * xor_roll(mixed, d, 1, lane, n)
        weights_t = ra * weights_t + rb * xor_roll(weights_t, d, 1, lane, n)
    return weights_t[:, 0:1]


def kernel(ctx_hbm, cot_hbm, out_hbm, out, ctx, cot, p, xr, blocks, pairs, lines, merged, g1, g2,
           load_sem, xs_sem, xr_sem, as_sem, ar_sem, gs_sem, gr_sem, near_sem, far_sem, core_sem,
           out_sem):
    n_rack, n_outer, n_tp = lax.axis_size("rack"), lax.axis_size("outer"), lax.axis_size("tp")
    k, o, t = lax.axis_index("rack"), lax.axis_index("outer"), lax.axis_index("tp")
    left, right, opp = (k + 3) % 4, (k + 1) % 4, (k + 2) % 4
    z, core = o // 2, o % 2
    zh, zl = z // 4, z % 4
    tok, width = ctx.shape
    half = width // 2
    rack_rows = p.shape[0] // 4
    rows48 = rack_rows // 16
    step_rows = 2 * rows48
    unit_rows = rack_rows // 2
    dest = (opp, right, left, k)

    def along_z(d):
        return {"outer": (z + d) % 8 * 2 + core}

    adjacent = [{"rack": left}, {"rack": right}, {"tp": (t + 1) % 4}, {"tp": (t + 3) % 4},
                along_z(1), along_z(7)]
    second = [{"rack": left}, {"rack": right}, {"rack": opp}, along_z(2), along_z(6)]
    barrier = pltpu.get_barrier_semaphore()
    for device in adjacent + [{"outer": o ^ 1}]:
        pl.semaphore_signal(barrier, inc=1, device_id=device, device_id_type=MESH)

    def greet(semaphore, devices):
        for device in devices:
            pl.semaphore_signal(semaphore, inc=1, device_id=device, device_id_type=MESH)

    def distance(s):
        odd = s % 2
        return (1 - odd) * (4 + s // 2) + odd * ((7 - s) // 2)

    def target(s):
        return (z + distance(s)) % 8

    def source(s):
        return (z + 8 - distance(s)) % 8

    def unit_cols(u):
        h = zh ^ (1 - u // 4)
        return dest[u % 4] * rack_rows + h * unit_rows

    def cot_load(u):
        cols = pl.ds(pl.multiple_of(unit_cols(u), 128), unit_rows)
        return pltpu.make_async_copy(cot_hbm.at[:, cols], cot.at[u], load_sem.at[u])

    def ctx_load(h):
        cols = pl.ds(h * half, half)
        return pltpu.make_async_copy(ctx_hbm.at[:, cols], ctx.at[:, cols], load_sem.at[8 + h])

    cot_load(0).start()
    for h in range(2):
        ctx_load(h).start()
    for u in range(1, 8):
        cot_load(u).start()

    def product(u, h):
        cols = pl.ds(pl.multiple_of(h * half, half), half)
        p[pl.ds(pl.multiple_of(unit_cols(u), 128), unit_rows), cols] = lax.dot_general(
            cot[u], ctx[:, cols], (((0,), (0,)), ((), ())),
            preferred_element_type=F32).astype(BF16)

    def unit(u):
        cot_load(u).wait()

        @pl.loop(0, 2)
        def _(h):
            product(u, h)

    lane_tiles = half // 128
    cuts = (0, lane_tiles // 2 * 128, lane_tiles * 5 // 6 * 128, half)
    pieces = [(s, 0, half) for s in range(7)]
    pieces += [(7, cuts[i], cuts[i + 1] - cuts[i]) for i in range(3)]

    def side(h, i):
        _, first, size = pieces[i]
        return pl.ds(h * half + first, size)

    def rows_of(j, s):
        return pl.ds(pl.multiple_of(j * rack_rows + target(s) * step_rows, 16), step_rows)

    def message(kind, i):
        s, first, size = pieces[i]
        j, h, to = (
            (opp, 0, left), (right, 0, right), (opp, 1, right), (left, 1, left),
            (left, 0, left), (right, 1, right))[kind]
        return pltpu.make_async_remote_copy(
            src_ref=p.at[rows_of(j, s), side(h, i)],
            dst_ref=xr.at[s, kind, :, pl.ds(first, size)],
            send_sem=xs_sem.at[i, kind],
            recv_sem=xr_sem.at[i, kind],
            device_id={"rack": to}, device_id_type=MESH)

    def add_into(j, h, i, kinds):
        s, first, size = pieces[i]
        rows = rows_of(j, s)

        @pl.loop(0, step_rows // 16)
        def _(r):
            here = pl.ds(pl.multiple_of(rows.start + r * 16, 16), 16)
            there = pl.ds(pl.multiple_of(r * 16, 16), 16)
            total = p[here, side(h, i)].astype(F32)
            for kind in kinds:
                total = total + xr[s, kind, there, pl.ds(first, size)].astype(F32)
            p[here, side(h, i)] = total.astype(BF16)

    def first_hops(i):
        for kind in (0, 2, 3, 1):
            message(kind, i).start()

    def relay(i):
        message(0, i).wait_recv()
        add_into(left, 0, i, (0,))
        message(4, i).start()
        message(2, i).wait_recv()
        add_into(right, 1, i, (2,))
        message(5, i).start()

    def slot(m):
        return pl.ds(pl.multiple_of(m * rows48, 16), rows48)

    def owner(m):
        return source(m // 2) * 2 + m % 2

    def block_send(s, c):
        to = target(s) * 2 + c
        start = k * rack_rows + target(s) * step_rows + c * rows48
        return pltpu.make_async_remote_copy(
            src_ref=p.at[pl.ds(pl.multiple_of(start, 16), rows48)],
            dst_ref=blocks.at[slot(2 * s + core)],
            send_sem=as_sem.at[s, c],
            recv_sem=ar_sem.at[2 * s + core],
            device_id={"outer": to}, device_id_type=MESH)

    def block_recv(m):
        return pltpu.make_async_remote_copy(
            src_ref=blocks.at[slot(m)], dst_ref=blocks.at[slot(m)], send_sem=as_sem.at[0, 0],
            recv_sem=ar_sem.at[m], device_id={"outer": owner(m)}, device_id_type=MESH)

    def peer_copy(h, i, m):
        start = k * rack_rows + (o ^ 1) * rows48
        return pltpu.make_async_remote_copy(
            src_ref=p.at[pl.ds(pl.multiple_of(start, 16), rows48), side(h, i)],
            dst_ref=blocks.at[slot(m), side(h, i)],
            send_sem=as_sem.at[i, h],
            recv_sem=ar_sem.at[n_outer + 2 * (i - 7) + h],
            device_id={"outer": o ^ 1}, device_id_type=MESH)

    def finish(i):
        s = pieces[i][0]
        for h, kinds in ((0, (1, 4)), (1, (3, 5))):
            for kind in kinds:
                message(kind, i).wait_recv()
            add_into(k, h, i, kinds)
            if s == 7:
                peer_copy(h, i, 14 + core).start()
        if s < 7:
            for c in range(2):
                block_send(s, c).start()
        else:
            start = pl.multiple_of(k * rack_rows + o * rows48, 16)
            for h in range(2):
                blocks[slot(14 + core), side(h, i)] = p[pl.ds(start, rows48), side(h, i)]

    def gram(i):
        s, first, size = pieces[i]
        if s < 7:
            for c in range(2):
                block_recv(2 * s + c).wait_recv()
        else:
            for h in range(2):
                peer_copy(h, i, 15 - core).wait_recv()
        count = 2 * s + 2
        newest = pl.ds(2 * s * rows48, step_rows)
        columns = (pl.ds(0, width),) if s < 7 else (side(0, i), side(1, i))
        products = 0.0
        for cols in columns:
            products = products + lax.dot_general(
                blocks[pl.ds(0, count * rows48), cols], blocks[newest, cols],
                (((1,), (1,)), ((), ())), preferred_element_type=F32)
        row = lax.broadcasted_iota(jnp.int32, (count, rows48, step_rows), 1)
        lane = lax.broadcasted_iota(jnp.int32, (count, rows48, step_rows), 2)
        mask = (row == lane) | (row + rows48 == lane)
        trace = jnp.sum(
            jnp.where(mask, products.reshape(count, rows48, step_rows), 0.0), axis=1)
        if first > 0:
            trace = trace + lines[...]
        if s == 7 and i < 9:
            lines[...] = trace
            return
        lane = lax.broadcasted_iota(jnp.int32, (count, step_rows), 1)
        for a in range(2):
            new = owner(2 * s + a)
            mine = jnp.where(lane // rows48 == a, trace, 0.0)
            for m in range(count):
                pairs[new, pl.ds(owner(m), 1), :] = mine[m:m + 1]
                if m < 2 * s:
                    pairs[owner(m), pl.ds(new, 1), :] = mine[m:m + 1]

    cot_load(0).wait()
    ctx_load(0).wait()
    product(0, 0)
    pl.semaphore_wait(barrier, 7)
    message(0, 0).start()
    greet(near_sem, adjacent)
    ctx_load(1).wait()
    product(0, 1)
    message(2, 0).start()
    unit(2)
    message(3, 0).start()
    unit(1)
    message(1, 0).start()
    pl.semaphore_wait(near_sem, 6)
    greet(far_sem, second)
    unit(4)
    message(0, 1).start()
    message(2, 1).start()
    relay(0)
    unit(6)
    message(3, 1).start()
    unit(5)
    message(1, 1).start()
    pl.semaphore_wait(far_sem, 5)
    greet(core_sem, [{"outer": o ^ 1}])
    first_hops(2)
    unit(3)
    unit(7)
    pl.semaphore_wait(core_sem, 1)
    for s in range(1, 7):
        relay(s)
        if s + 2 < 7:
            first_hops(s + 2)
        if s == 6:
            for kinds in ((0, 2), (3, 1)):
                for i in (7, 8, 9):
                    for kind in kinds:
                        message(kind, i).start()
        finish(s - 1)
        if s >= 3:
            gram(s - 3)
    finish(6)
    for i in (7, 8, 9):
        relay(i)
    gram(4)
    gram(5)
    finish(7)
    gram(6)
    finish(8)
    finish(9)
    gram(7)
    gram(8)
    gram(9)

    rowsum = jnp.sum(pairs[...], axis=2, keepdims=True)
    j_index = lax.broadcasted_iota(jnp.int32, (n_outer, n_outer, 128), 1)
    lanes = lax.broadcasted_iota(jnp.int32, (n_outer, n_outer, 128), 2)
    me1 = k * n_tp + t
    g1[me1] = jnp.sum(jnp.where(j_index == lanes, rowsum, 0.0), axis=1)

    def share1(d):
        to_k, to_t = (k + d // n_tp) % n_rack, (t + d % n_tp) % n_tp
        return pltpu.make_async_remote_copy(
            src_ref=g1.at[me1], dst_ref=g1.at[me1], send_sem=gs_sem.at[0, d],
            recv_sem=gr_sem.at[0, me1], device_id={"rack": to_k, "tp": to_t}, device_id_type=MESH)

    def share1_recv(d):
        from_k, from_t = (k + d // n_tp) % n_rack, (t + d % n_tp) % n_tp
        q = from_k * n_tp + from_t
        return pltpu.make_async_remote_copy(
            src_ref=g1.at[q], dst_ref=g1.at[q], send_sem=gs_sem.at[0, d],
            recv_sem=gr_sem.at[0, q], device_id={"rack": from_k, "tp": from_t}, device_id_type=MESH)

    def hops(d):
        return min(d // n_tp, n_rack - d // n_tp) + min(d % n_tp, n_tp - d % n_tp)

    for d in sorted(range(1, n_rack * n_tp), key=hops, reverse=True):
        share1(d).start()
    for i in range(10):
        for kind in range(6):
            message(kind, i).wait_send()
        for h in range(2):
            if i < 7:
                block_send(i, h).wait_send()
            else:
                peer_copy(h, i, 14 + core).wait_send()
    for d in range(1, n_rack * n_tp):
        share1_recv(d).wait_recv()
    g2[o] = jnp.sum(g1[...], axis=0)

    def share2(d):
        return pltpu.make_async_remote_copy(
            src_ref=g2.at[o], dst_ref=g2.at[o], send_sem=gs_sem.at[1, d],
            recv_sem=gr_sem.at[1, o], device_id={"outer": (o + d) % n_outer}, device_id_type=MESH)

    def share2_recv(d):
        q = (o + d) % n_outer
        return pltpu.make_async_remote_copy(
            src_ref=g2.at[q], dst_ref=g2.at[q], send_sem=gs_sem.at[1, d],
            recv_sem=gr_sem.at[1, q], device_id={"outer": q}, device_id_type=MESH)

    for d in sorted(range(1, n_outer), key=lambda d: abs(2 * d - n_outer)):
        share2(d).start()
    for d in range(1, n_outer):
        share2_recv(d).wait_recv()
    weights = merge_weights(jnp.sum(g2[...], axis=0), n_outer, 4)

    merged[...] = jnp.broadcast_to(weights, merged.shape)
    spread = [
        jnp.broadcast_to(merged[pl.ds(owner(m), 1), :], (16, 128)) for m in range(n_outer)]

    def out_copy(r):
        rows = pl.ds(r * 16, 16)
        return pltpu.make_async_copy(out.at[rows], out_hbm.at[rows], out_sem.at[r])

    for r in range(rows48 // 16):
        for c in range(width // 128):
            cols = pl.ds(c * 128, 128)
            total = 0.0
            for m in range(n_outer):
                rows = pl.ds(m * rows48 + r * 16, 16)
                total = total + spread[m] * blocks[rows, cols].astype(F32)
            out[pl.ds(r * 16, 16), cols] = total.astype(BF16)
        out_copy(r).start()
    for r in range(rows48 // 16):
        out_copy(r).wait()

    for d in range(1, n_rack * n_tp):
        share1(d).wait_send()
    for d in range(1, n_outer):
        share2(d).wait_send()


def shards(context, cotangent):
    tok, width = context.shape
    cols = cotangent.shape[1]
    n_outer = lax.axis_size("outer")
    rack_rows = cols // 4
    rows48 = rack_rows // 16
    return pl.pallas_call(
        kernel,
        out_shape=jax.ShapeDtypeStruct((rows48, width), BF16),
        in_specs=[pl.BlockSpec(memory_space=pl.ANY)] * 2,
        out_specs=pl.BlockSpec(memory_space=pl.ANY),
        scratch_shapes=[
            pltpu.VMEM((rows48, width), BF16),
            pltpu.VMEM((tok, width), BF16),
            pltpu.VMEM((8, tok, rack_rows // 2), BF16),
            pltpu.VMEM((cols, width), BF16),
            pltpu.VMEM((8, 6, 2 * rows48, width // 2), BF16),
            pltpu.VMEM((n_outer * rows48, width), BF16),
            pltpu.VMEM((n_outer, n_outer, 2 * rows48), F32),
            pltpu.VMEM((n_outer, 2 * rows48), F32),
            pltpu.VMEM((n_outer, 128), F32),
            pltpu.VMEM((16, n_outer, 128), F32),
            pltpu.VMEM((16, n_outer, 128), F32),
            pltpu.SemaphoreType.DMA((10,)),
            pltpu.SemaphoreType.DMA((10, 6)),
            pltpu.SemaphoreType.DMA((10, 6)),
            pltpu.SemaphoreType.DMA((10, 2)),
            pltpu.SemaphoreType.DMA((22,)),
            pltpu.SemaphoreType.DMA((2, 16)),
            pltpu.SemaphoreType.DMA((2, 16)),
            pltpu.SemaphoreType.REGULAR,
            pltpu.SemaphoreType.REGULAR,
            pltpu.SemaphoreType.REGULAR,
            pltpu.SemaphoreType.DMA((rows48 // 16,)),
        ],
        compiler_params=pltpu.CompilerParams(
            collective_id=0, has_side_effects=True, vmem_limit_bytes=56 * 2**20),
    )(context, cotangent)


def solution(mesh):
    return jax.shard_map(
        shards,
        mesh=mesh,
        in_specs=(P(("rack", "outer"), "tp"), P(("rack", "outer"), None)),
        out_specs=P(("rack", "outer"), "tp"),
        check_vma=False,
    )
```

```python
import functools
import jax
import jax.numpy as jnp
from jax import lax
from jax.experimental import pallas as pl
from jax.experimental.pallas import tpu as pltpu
from jax.sharding import PartitionSpec as P

EPS = 1e-06
MESH = pl.DeviceIdType.MESH
F32 = jnp.float32
BF16 = jnp.bfloat16


def xor_roll(x, distance, axis, index, size):
    up = pltpu.roll(x, x.shape[axis] - distance, axis)
    down = pltpu.roll(x, distance, axis)
    return jnp.where((index & distance) == 0, up, down)


def merge_weights(gram, n, levels):
    row = lax.broadcasted_iota(jnp.int32, gram.shape, 0)
    lane = lax.broadcasted_iota(jnp.int32, gram.shape, 1)
    diagonal = row == lane
    weights_t = jnp.where(diagonal, 1.0, 0.0).astype(F32)

    def mixing(aa, bb, ab):
        aa, bb = jnp.maximum(aa, 0.0), jnp.maximum(bb, 0.0)
        bound = jnp.sqrt(aa) * jnp.sqrt(bb)
        ab = jnp.clip(ab, -bound, bound)
        return 1.0 - ab / (2.0 * (aa + EPS)), 1.0 - ab / (2.0 * (bb + EPS))

    for level in range(levels):
        d = 1 << level
        partner = (row ^ d) == lane
        gram_r = xor_roll(gram, d, 0, row, n)
        gram_l = xor_roll(gram, d, 1, lane, n)

        def column(x, mask):
            return jnp.sum(jnp.where(mask, x, 0.0), axis=1, keepdims=True)

        def line(x, mask):
            return jnp.sum(jnp.where(mask, x, 0.0), axis=0, keepdims=True)

        ca, cb = mixing(column(gram, diagonal), column(gram_r, partner), column(gram, partner))
        ra, rb = mixing(line(gram, diagonal), line(gram_l, partner), line(gram, partner))
        mixed = ca * gram + cb * gram_r
        gram = ra * mixed + rb * xor_roll(mixed, d, 1, lane, n)
        weights_t = ra * weights_t + rb * xor_roll(weights_t, d, 1, lane, n)
    return weights_t[:, 0:1]


def kernel(ctx_hbm, cot_hbm, out_hbm, out, ctx, cot, p, xr, xq, blocks, pairs, lines, merged, g1, g2,
           load_sem, xs_sem, xr_sem, as_sem, ar_sem, gs_sem, gr_sem, near_sem, far_sem, core_sem,
           out_sem, ps_sem, pr_sem, os_sem, or_sem):
    n_rack, n_outer, n_tp = lax.axis_size("rack"), lax.axis_size("outer"), lax.axis_size("tp")
    k, o, t = lax.axis_index("rack"), lax.axis_index("outer"), lax.axis_index("tp")
    left, right, opp = (k + 3) % 4, (k + 1) % 4, (k + 2) % 4
    z, core = o // 2, o % 2
    zh, zl = z // 4, z % 4
    tok, width = ctx.shape
    half = width // 2
    rack_rows = p.shape[0] // 4
    rows48 = rack_rows // 16
    step_rows = 2 * rows48
    unit_rows = rack_rows // 2
    dest = (opp, right, left, k)

    def along_z(d):
        return {"outer": (z + d) % 8 * 2 + core}

    adjacent = [{"rack": left}, {"rack": right}, {"tp": (t + 1) % 4}, {"tp": (t + 3) % 4},
                along_z(1), along_z(7)]
    second = [{"rack": left}, {"rack": right}, {"rack": opp}, along_z(2), along_z(6)]
    barrier = pltpu.get_barrier_semaphore()
    for device in adjacent + [{"outer": o ^ 1}]:
        pl.semaphore_signal(barrier, inc=1, device_id=device, device_id_type=MESH)

    def greet(semaphore, devices):
        for device in devices:
            pl.semaphore_signal(semaphore, inc=1, device_id=device, device_id_type=MESH)

    def distance(s):
        odd = s % 2
        return (1 - odd) * (4 + s // 2) + odd * ((7 - s) // 2)

    def target(s):
        return (z + distance(s)) % 8

    def source(s):
        return (z + 8 - distance(s)) % 8

    def unit_cols(u):
        h = zh ^ (1 - u // 4)
        return dest[u % 4] * rack_rows + h * unit_rows

    def cot_load(u):
        cols = pl.ds(pl.multiple_of(unit_cols(u), 128), unit_rows)
        return pltpu.make_async_copy(cot_hbm.at[:, cols], cot.at[u], load_sem.at[u])

    def ctx_load(h):
        cols = pl.ds(h * half, half)
        return pltpu.make_async_copy(ctx_hbm.at[:, cols], ctx.at[:, cols], load_sem.at[8 + h])

    cot_load(0).start()
    for h in range(2):
        ctx_load(h).start()
    for u in range(1, 8):
        cot_load(u).start()

    def product(u, h, parts=1, part=0):
        size = half // parts
        cols = pl.ds(pl.multiple_of(h * half + part * size, size), size)
        p[pl.ds(pl.multiple_of(unit_cols(u), 128), unit_rows), cols] = lax.dot_general(
            cot[u], ctx[:, cols], (((0,), (0,)), ((), ())),
            preferred_element_type=F32).astype(BF16)

    def unit(u):
        cot_load(u).wait()

        @pl.loop(0, 2)
        def _(h):
            product(u, h)

    lane_tiles = half // 128
    cuts = (0, lane_tiles // 2 * 128, lane_tiles * 5 // 6 * 128, half)
    pieces = [(s, 0, half) for s in range(7)]
    pieces += [(7, cuts[i], cuts[i + 1] - cuts[i]) for i in range(3)]

    def side(h, i):
        _, first, size = pieces[i]
        return pl.ds(h * half + first, size)

    def rows_of(j, s):
        return pl.ds(pl.multiple_of(j * rack_rows + target(s) * step_rows, 16), step_rows)

    def rows_for(j, group):
        return pl.ds(pl.multiple_of(j * rack_rows + group * rows48, 16), rows48)

    def message(kind, i):
        s, first, size = pieces[i]
        j, h, to = (
            (opp, 0, left), (right, 0, right), (opp, 1, right), (left, 1, left),
            (left, 0, left), (right, 1, right))[kind]
        rows, there = rows_of(j, s), pl.ds(0, step_rows)
        if i == 9 and kind >= 4:
            rows, there = rows_for(j, o), pl.ds(pl.multiple_of(core * rows48, 16), rows48)
        return pltpu.make_async_remote_copy(
            src_ref=p.at[rows, side(h, i)],
            dst_ref=xr.at[s, kind, there, pl.ds(first, size)],
            send_sem=xs_sem.at[i, kind],
            recv_sem=xr_sem.at[i, kind],
            device_id={"rack": to}, device_id_type=MESH)

    def passed(h):
        j = (left, right)[h]
        return pltpu.make_async_remote_copy(
            src_ref=p.at[rows_for(j, o ^ 1), side(h, 9)],
            dst_ref=xq.at[h],
            send_sem=ps_sem.at[h],
            recv_sem=pr_sem.at[h],
            device_id={"rack": j, "outer": o ^ 1}, device_id_type=MESH)

    def add_into(j, h, i, kinds):
        s, first, size = pieces[i]
        rows = rows_of(j, s)

        @pl.loop(0, step_rows // 16)
        def _(r):
            here = pl.ds(pl.multiple_of(rows.start + r * 16, 16), 16)
            there = pl.ds(pl.multiple_of(r * 16, 16), 16)
            total = p[here, side(h, i)].astype(F32)
            for kind in kinds:
                total = total + xr[s, kind, there, pl.ds(first, size)].astype(F32)
            p[here, side(h, i)] = total.astype(BF16)

    def opening(h, c):
        cols = pl.ds(c * (half // 2), half // 2)
        return pltpu.make_async_remote_copy(
            src_ref=p.at[rows_of(opp, 0), pl.ds(h * half + c * (half // 2), half // 2)],
            dst_ref=xr.at[0, 2 * h, :, cols],
            send_sem=os_sem.at[h, c],
            recv_sem=or_sem.at[h, c],
            device_id={"rack": (left, right)[h]}, device_id_type=MESH)

    def arrived(h, i):
        if i == 0:
            for c in range(2):
                opening(h, c).wait_recv()
        else:
            message(2 * h, i).wait_recv()

    def first_hops(i):
        for kind in (0, 2, 3, 1):
            message(kind, i).start()

    def relay(i):
        arrived(0, i)
        add_into(left, 0, i, (0,))
        message(4, i).start()
        if i == 9:
            passed(0).start()
        arrived(1, i)
        add_into(right, 1, i, (2,))
        message(5, i).start()
        if i == 9:
            passed(1).start()

    def slot(m):
        return pl.ds(pl.multiple_of(m * rows48, 16), rows48)

    def owner(m):
        return source(m // 2) * 2 + m % 2

    def block_send(s, c):
        to = target(s) * 2 + c
        start = k * rack_rows + target(s) * step_rows + c * rows48
        return pltpu.make_async_remote_copy(
            src_ref=p.at[pl.ds(pl.multiple_of(start, 16), rows48)],
            dst_ref=blocks.at[slot(2 * s + core)],
            send_sem=as_sem.at[s, c],
            recv_sem=ar_sem.at[2 * s + core],
            device_id={"outer": to}, device_id_type=MESH)

    def block_recv(m):
        return pltpu.make_async_remote_copy(
            src_ref=blocks.at[slot(m)], dst_ref=blocks.at[slot(m)], send_sem=as_sem.at[0, 0],
            recv_sem=ar_sem.at[m], device_id={"outer": owner(m)}, device_id_type=MESH)

    def peer_copy(h, i, m):
        start = k * rack_rows + (o ^ 1) * rows48
        return pltpu.make_async_remote_copy(
            src_ref=p.at[pl.ds(pl.multiple_of(start, 16), rows48), side(h, i)],
            dst_ref=blocks.at[slot(m), side(h, i)],
            send_sem=as_sem.at[i, h],
            recv_sem=ar_sem.at[n_outer + 2 * (i - 7) + h],
            device_id={"outer": o ^ 1}, device_id_type=MESH)

    def finish(i):
        s = pieces[i][0]
        for h, kinds in ((0, (1, 4)), (1, (3, 5))):
            for kind in kinds:
                message(kind, i).wait_recv()
            add_into(k, h, i, kinds)
            if s == 7:
                peer_copy(h, i, 14 + core).start()
        if s < 7:
            for c in range(2):
                block_send(s, c).start()
        else:
            start = pl.multiple_of(k * rack_rows + o * rows48, 16)
            for h in range(2):
                blocks[slot(14 + core), side(h, i)] = p[pl.ds(start, rows48), side(h, i)]

    def finish_last():
        first, size = pieces[9][1:]
        cols = pl.ds(first, size)
        mine = pl.ds(pl.multiple_of(core * rows48, 16), rows48)
        theirs = pl.ds(pl.multiple_of((1 - core) * rows48, 16), rows48)
        for h, kind in ((0, 1), (1, 3)):
            message(kind, 9).wait_recv()
            rows = rows_for(k, o ^ 1)
            total = p[rows, side(h, 9)].astype(F32) + xr[7, kind, theirs, cols].astype(F32)
            p[rows, side(h, 9)] = total.astype(BF16)
            peer_copy(h, 9, 14 + core).start()
        for h, kind in ((0, 1), (1, 3)):
            message(kind // 2 + 4, 9).wait_recv()
            total = p[rows_for(k, o), side(h, 9)].astype(F32)
            for part in (kind, kind // 2 + 4):
                total = total + xr[7, part, mine, cols].astype(F32)
            blocks[slot(14 + core), side(h, 9)] = total.astype(BF16)

    def gram(i):
        s, first = pieces[i][:2]
        if s < 7:
            for c in range(2):
                block_recv(2 * s + c).wait_recv()
        else:
            for h in range(2):
                for part in ((7,) if i == 7 else (8, 9)):
                    peer_copy(h, part, 15 - core).wait_recv()
                if i == 8:
                    passed(h).wait_recv()
                    here = slot(15 - core)
                    total = blocks[here, side(h, 9)].astype(F32) + xq[h].astype(F32)
                    blocks[here, side(h, 9)] = total.astype(BF16)
        count = 2 * s + 2
        newest = pl.ds(2 * s * rows48, step_rows)
        columns = (pl.ds(0, width),)
        if s == 7:
            size = cuts[1] if i == 7 else half - cuts[1]
            columns = tuple(pl.ds(h * half + first, size) for h in range(2))
        products = 0.0
        for cols in columns:
            products = products + lax.dot_general(
                blocks[pl.ds(0, count * rows48), cols], blocks[newest, cols],
                (((1,), (1,)), ((), ())), preferred_element_type=F32)
        row = lax.broadcasted_iota(jnp.int32, (count, rows48, step_rows), 1)
        lane = lax.broadcasted_iota(jnp.int32, (count, rows48, step_rows), 2)
        mask = (row == lane) | (row + rows48 == lane)
        trace = jnp.sum(
            jnp.where(mask, products.reshape(count, rows48, step_rows), 0.0), axis=1)
        if first > 0:
            trace = trace + lines[...]
        if i == 7:
            lines[...] = trace
            return
        lane = lax.broadcasted_iota(jnp.int32, (count, step_rows), 1)
        for a in range(2):
            new = owner(2 * s + a)
            mine = jnp.where(lane // rows48 == a, trace, 0.0)
            for m in range(count):
                pairs[new, pl.ds(owner(m), 1), :] = mine[m:m + 1]
                if m < 2 * s:
                    pairs[owner(m), pl.ds(new, 1), :] = mine[m:m + 1]

    cot_load(0).wait()
    ctx_load(0).wait()
    product(0, 0, 2, 0)
    pl.semaphore_wait(barrier, 7)
    opening(0, 0).start()
    ctx_load(1).wait()
    product(0, 1, 2, 0)
    opening(1, 0).start()
    product(0, 0, 2, 1)
    opening(0, 1).start()
    product(0, 1, 2, 1)
    opening(1, 1).start()
    greet(near_sem, adjacent)
    cot_load(2).wait()
    product(2, 1)
    message(3, 0).start()
    cot_load(1).wait()
    product(1, 0)
    message(1, 0).start()
    pl.semaphore_wait(near_sem, 6)
    greet(far_sem, second)
    cot_load(4).wait()
    product(4, 0)
    message(0, 1).start()
    product(4, 1)
    message(2, 1).start()
    product(2, 0)
    product(1, 1)
    relay(0)
    cot_load(6).wait()
    product(6, 1)
    message(3, 1).start()
    cot_load(5).wait()
    product(5, 0)
    message(1, 1).start()
    product(6, 0)
    product(5, 1)
    pl.semaphore_wait(far_sem, 5)
    greet(core_sem, [{"outer": o ^ 1}])
    first_hops(2)
    unit(3)
    unit(7)
    pl.semaphore_wait(core_sem, 1)
    for s in range(1, 7):
        relay(s)
        if s + 2 < 7:
            first_hops(s + 2)
        if s == 6:
            for kinds in ((0, 2), (3, 1)):
                for i in (7, 8, 9):
                    for kind in kinds:
                        message(kind, i).start()
        finish(s - 1)
        if s >= 3:
            gram(s - 3)
    finish(6)
    for i in (7, 8, 9):
        relay(i)
    gram(4)
    gram(5)
    finish(7)
    gram(6)
    finish(8)
    finish_last()
    gram(7)
    gram(8)

    rowsum = jnp.sum(pairs[...], axis=2, keepdims=True)
    j_index = lax.broadcasted_iota(jnp.int32, (n_outer, n_outer, 128), 1)
    lanes = lax.broadcasted_iota(jnp.int32, (n_outer, n_outer, 128), 2)
    me1 = k * n_tp + t
    g1[me1] = jnp.sum(jnp.where(j_index == lanes, rowsum, 0.0), axis=1)

    def share1(d):
        to_k, to_t = (k + d // n_tp) % n_rack, (t + d % n_tp) % n_tp
        return pltpu.make_async_remote_copy(
            src_ref=g1.at[me1], dst_ref=g1.at[me1], send_sem=gs_sem.at[0, d],
            recv_sem=gr_sem.at[0, me1], device_id={"rack": to_k, "tp": to_t}, device_id_type=MESH)

    def share1_recv(d):
        from_k, from_t = (k + d // n_tp) % n_rack, (t + d % n_tp) % n_tp
        q = from_k * n_tp + from_t
        return pltpu.make_async_remote_copy(
            src_ref=g1.at[q], dst_ref=g1.at[q], send_sem=gs_sem.at[0, d],
            recv_sem=gr_sem.at[0, q], device_id={"rack": from_k, "tp": from_t}, device_id_type=MESH)

    def hops(d):
        return min(d // n_tp, n_rack - d // n_tp) + min(d % n_tp, n_tp - d % n_tp)

    for d in sorted(range(1, n_rack * n_tp), key=hops, reverse=True):
        share1(d).start()
    for i in range(10):
        for kind in range(6):
            if i == 0 and kind in (0, 2):
                for c in range(2):
                    opening(kind // 2, c).wait_send()
            else:
                message(kind, i).wait_send()
        for h in range(2):
            if i < 7:
                block_send(i, h).wait_send()
            else:
                peer_copy(h, i, 14 + core).wait_send()
    for h in range(2):
        passed(h).wait_send()
    for d in range(1, n_rack * n_tp):
        share1_recv(d).wait_recv()
    g2[o] = jnp.sum(g1[...], axis=0)

    def share2(d):
        return pltpu.make_async_remote_copy(
            src_ref=g2.at[o], dst_ref=g2.at[o], send_sem=gs_sem.at[1, d],
            recv_sem=gr_sem.at[1, o], device_id={"outer": (o + d) % n_outer}, device_id_type=MESH)

    def share2_recv(d):
        q = (o + d) % n_outer
        return pltpu.make_async_remote_copy(
            src_ref=g2.at[q], dst_ref=g2.at[q], send_sem=gs_sem.at[1, d],
            recv_sem=gr_sem.at[1, q], device_id={"outer": q}, device_id_type=MESH)

    for d in sorted(range(1, n_outer), key=lambda d: abs(2 * d - n_outer)):
        share2(d).start()
    for d in range(1, n_outer):
        share2_recv(d).wait_recv()
    weights = merge_weights(jnp.sum(g2[...], axis=0), n_outer, 4)

    merged[...] = jnp.broadcast_to(weights, merged.shape)
    spread = [
        jnp.broadcast_to(merged[pl.ds(owner(m), 1), :], (16, 128)) for m in range(n_outer)]

    def out_copy(r):
        rows = pl.ds(r * 16, 16)
        return pltpu.make_async_copy(out.at[rows], out_hbm.at[rows], out_sem.at[r])

    for r in range(rows48 // 16):
        for c in range(width // 128):
            cols = pl.ds(c * 128, 128)
            total = 0.0
            for m in range(n_outer):
                rows = pl.ds(m * rows48 + r * 16, 16)
                total = total + spread[m] * blocks[rows, cols].astype(F32)
            out[pl.ds(r * 16, 16), cols] = total.astype(BF16)
        out_copy(r).start()
    for r in range(rows48 // 16):
        out_copy(r).wait()

    for d in range(1, n_rack * n_tp):
        share1(d).wait_send()
    for d in range(1, n_outer):
        share2(d).wait_send()


def shards(context, cotangent):
    tok, width = context.shape
    cols = cotangent.shape[1]
    n_outer = lax.axis_size("outer")
    rack_rows = cols // 4
    rows48 = rack_rows // 16
    return pl.pallas_call(
        kernel,
        out_shape=jax.ShapeDtypeStruct((rows48, width), BF16),
        in_specs=[pl.BlockSpec(memory_space=pl.ANY)] * 2,
        out_specs=pl.BlockSpec(memory_space=pl.ANY),
        scratch_shapes=[
            pltpu.VMEM((rows48, width), BF16),
            pltpu.VMEM((tok, width), BF16),
            pltpu.VMEM((8, tok, rack_rows // 2), BF16),
            pltpu.VMEM((cols, width), BF16),
            pltpu.VMEM((8, 6, 2 * rows48, width // 2), BF16),
            pltpu.VMEM((2, rows48, width // 12), BF16),
            pltpu.VMEM((n_outer * rows48, width), BF16),
            pltpu.VMEM((n_outer, n_outer, 2 * rows48), F32),
            pltpu.VMEM((n_outer, 2 * rows48), F32),
            pltpu.VMEM((n_outer, 128), F32),
            pltpu.VMEM((16, n_outer, 128), F32),
            pltpu.VMEM((16, n_outer, 128), F32),
            pltpu.SemaphoreType.DMA((10,)),
            pltpu.SemaphoreType.DMA((10, 6)),
            pltpu.SemaphoreType.DMA((10, 6)),
            pltpu.SemaphoreType.DMA((10, 2)),
            pltpu.SemaphoreType.DMA((22,)),
            pltpu.SemaphoreType.DMA((2, 16)),
            pltpu.SemaphoreType.DMA((2, 16)),
            pltpu.SemaphoreType.REGULAR,
            pltpu.SemaphoreType.REGULAR,
            pltpu.SemaphoreType.REGULAR,
            pltpu.SemaphoreType.DMA((rows48 // 16,)),
            pltpu.SemaphoreType.DMA((2,)),
            pltpu.SemaphoreType.DMA((2,)),
            pltpu.SemaphoreType.DMA((2, 2)),
            pltpu.SemaphoreType.DMA((2, 2)),
        ],
        compiler_params=pltpu.CompilerParams(
            collective_id=0, has_side_effects=True, vmem_limit_bytes=56 * 2**20),
    )(context, cotangent)


def solution(mesh):
    return jax.shard_map(
        shards,
        mesh=mesh,
        in_specs=(P(("rack", "outer"), "tp"), P(("rack", "outer"), None)),
        out_specs=P(("rack", "outer"), "tp"),
        check_vma=False,
    )
```

```python
import functools
import jax
import jax.numpy as jnp
from jax import lax
from jax.experimental import pallas as pl
from jax.experimental.pallas import tpu as pltpu
from jax.sharding import PartitionSpec as P

EPS = 1e-06
MESH = pl.DeviceIdType.MESH
F32 = jnp.float32
BF16 = jnp.bfloat16


def xor_roll(x, distance, axis, index, size):
    up = pltpu.roll(x, x.shape[axis] - distance, axis)
    down = pltpu.roll(x, distance, axis)
    return jnp.where((index & distance) == 0, up, down)


def merge_weights(gram, n, levels):
    row = lax.broadcasted_iota(jnp.int32, gram.shape, 0)
    lane = lax.broadcasted_iota(jnp.int32, gram.shape, 1)
    diagonal = row == lane
    weights_t = jnp.where(diagonal, 1.0, 0.0).astype(F32)

    def mixing(aa, bb, ab):
        aa, bb = jnp.maximum(aa, 0.0), jnp.maximum(bb, 0.0)
        bound = jnp.sqrt(aa) * jnp.sqrt(bb)
        ab = jnp.clip(ab, -bound, bound)
        return 1.0 - ab / (2.0 * (aa + EPS)), 1.0 - ab / (2.0 * (bb + EPS))

    for level in range(levels):
        d = 1 << level
        partner = (row ^ d) == lane
        gram_r = xor_roll(gram, d, 0, row, n)
        gram_l = xor_roll(gram, d, 1, lane, n)

        def column(x, mask):
            return jnp.sum(jnp.where(mask, x, 0.0), axis=1, keepdims=True)

        def line(x, mask):
            return jnp.sum(jnp.where(mask, x, 0.0), axis=0, keepdims=True)

        ca, cb = mixing(column(gram, diagonal), column(gram_r, partner), column(gram, partner))
        ra, rb = mixing(line(gram, diagonal), line(gram_l, partner), line(gram, partner))
        mixed = ca * gram + cb * gram_r
        gram = ra * mixed + rb * xor_roll(mixed, d, 1, lane, n)
        weights_t = ra * weights_t + rb * xor_roll(weights_t, d, 1, lane, n)
    return weights_t[:, 0:1]


def kernel(ctx_hbm, cot_hbm, out_hbm, out, ctx, cot, p, xr, xq, blocks, pairs, lines, merged, g1, g2,
           load_sem, xs_sem, xr_sem, as_sem, ar_sem, gs_sem, gr_sem, near_sem, far_sem, core_sem,
           out_sem, ps_sem, pr_sem, os_sem, or_sem):
    n_rack, n_outer, n_tp = lax.axis_size("rack"), lax.axis_size("outer"), lax.axis_size("tp")
    k, o, t = lax.axis_index("rack"), lax.axis_index("outer"), lax.axis_index("tp")
    left, right, opp = (k + 3) % 4, (k + 1) % 4, (k + 2) % 4
    z, core = o // 2, o % 2
    zh, zl = z // 4, z % 4
    tok, width = ctx.shape
    half = width // 2
    rack_rows = p.shape[0] // 4
    rows48 = rack_rows // 16
    step_rows = 2 * rows48
    unit_rows = rack_rows // 2
    dest = (opp, right, left, k)

    def along_z(d):
        return {"outer": (z + d) % 8 * 2 + core}

    adjacent = [{"rack": left}, {"rack": right}, {"tp": (t + 1) % 4}, {"tp": (t + 3) % 4},
                along_z(1), along_z(7)]
    second = [{"rack": left}, {"rack": right}, {"rack": opp}, along_z(2), along_z(6)]
    barrier = pltpu.get_barrier_semaphore()
    for device in adjacent + [{"outer": o ^ 1}]:
        pl.semaphore_signal(barrier, inc=1, device_id=device, device_id_type=MESH)

    def greet(semaphore, devices):
        for device in devices:
            pl.semaphore_signal(semaphore, inc=1, device_id=device, device_id_type=MESH)

    def distance(s):
        odd = s % 2
        return (1 - odd) * (4 + s // 2) + odd * ((7 - s) // 2)

    def target(s):
        return (z + distance(s)) % 8

    def source(s):
        return (z + 8 - distance(s)) % 8

    def unit_cols(u):
        h = zh ^ (1 - u // 4)
        return dest[u % 4] * rack_rows + h * unit_rows

    def cot_load(u):
        cols = pl.ds(pl.multiple_of(unit_cols(u), 128), unit_rows)
        return pltpu.make_async_copy(cot_hbm.at[:, cols], cot.at[u], load_sem.at[u])

    def ctx_load(h):
        cols = pl.ds(h * half, half)
        return pltpu.make_async_copy(ctx_hbm.at[:, cols], ctx.at[:, cols], load_sem.at[8 + h])

    cot_load(0).start()
    for h in range(2):
        ctx_load(h).start()
    for u in range(1, 8):
        cot_load(u).start()

    def product(u, h, parts=1, part=0):
        size = half // parts
        cols = pl.ds(pl.multiple_of(h * half + part * size, size), size)
        p[pl.ds(pl.multiple_of(unit_cols(u), 128), unit_rows), cols] = lax.dot_general(
            cot[u], ctx[:, cols], (((0,), (0,)), ((), ())),
            preferred_element_type=F32).astype(BF16)

    def unit(u):
        cot_load(u).wait()

        @pl.loop(0, 2)
        def _(h):
            product(u, h)

    lane_tiles = half // 128
    cuts = (0, lane_tiles // 2 * 128, lane_tiles * 5 // 6 * 128, half)
    pieces = [(s, 0, half) for s in range(7)]
    pieces += [(7, cuts[i], cuts[i + 1] - cuts[i]) for i in range(3)]

    def side(h, i):
        _, first, size = pieces[i]
        return pl.ds(h * half + first, size)

    def rows_of(j, s):
        return pl.ds(pl.multiple_of(j * rack_rows + target(s) * step_rows, 16), step_rows)

    def rows_for(j, group):
        return pl.ds(pl.multiple_of(j * rack_rows + group * rows48, 16), rows48)

    def message(kind, i):
        s, first, size = pieces[i]
        j, h, to = (
            (opp, 0, left), (right, 0, right), (opp, 1, right), (left, 1, left),
            (left, 0, left), (right, 1, right))[kind]
        rows, there = rows_of(j, s), pl.ds(0, step_rows)
        if i == 9 and kind >= 4:
            rows, there = rows_for(j, o), pl.ds(pl.multiple_of(core * rows48, 16), rows48)
        return pltpu.make_async_remote_copy(
            src_ref=p.at[rows, side(h, i)],
            dst_ref=xr.at[s, kind, there, pl.ds(first, size)],
            send_sem=xs_sem.at[i, kind],
            recv_sem=xr_sem.at[i, kind],
            device_id={"rack": to}, device_id_type=MESH)

    def passed(h):
        j = (left, right)[h]
        return pltpu.make_async_remote_copy(
            src_ref=p.at[rows_for(j, o ^ 1), side(h, 9)],
            dst_ref=xq.at[h],
            send_sem=ps_sem.at[h],
            recv_sem=pr_sem.at[h],
            device_id={"rack": j, "outer": o ^ 1}, device_id_type=MESH)

    def add_into(j, h, i, kinds):
        s, first, size = pieces[i]
        rows = rows_of(j, s)

        @pl.loop(0, step_rows // 16)
        def _(r):
            here = pl.ds(pl.multiple_of(rows.start + r * 16, 16), 16)
            there = pl.ds(pl.multiple_of(r * 16, 16), 16)
            total = p[here, side(h, i)].astype(F32)
            for kind in kinds:
                total = total + xr[s, kind, there, pl.ds(first, size)].astype(F32)
            p[here, side(h, i)] = total.astype(BF16)

    def opening(h, c):
        cols = pl.ds(c * (half // 2), half // 2)
        return pltpu.make_async_remote_copy(
            src_ref=p.at[rows_of(opp, 0), pl.ds(h * half + c * (half // 2), half // 2)],
            dst_ref=xr.at[0, 2 * h, :, cols],
            send_sem=os_sem.at[h, c],
            recv_sem=or_sem.at[h, c],
            device_id={"rack": (left, right)[h]}, device_id_type=MESH)

    def arrived(h, i):
        if i == 0:
            for c in range(2):
                opening(h, c).wait_recv()
        else:
            message(2 * h, i).wait_recv()

    def first_hops(i):
        for kind in (0, 2, 3, 1):
            message(kind, i).start()

    def relay(i):
        arrived(0, i)
        add_into(left, 0, i, (0,))
        message(4, i).start()
        if i == 9:
            passed(0).start()
        arrived(1, i)
        add_into(right, 1, i, (2,))
        message(5, i).start()
        if i == 9:
            passed(1).start()

    def slot(m):
        return pl.ds(pl.multiple_of(m * rows48, 16), rows48)

    def owner(m):
        return source(m // 2) * 2 + m % 2

    def block_send(s, c):
        to = target(s) * 2 + c
        start = k * rack_rows + target(s) * step_rows + c * rows48
        return pltpu.make_async_remote_copy(
            src_ref=p.at[pl.ds(pl.multiple_of(start, 16), rows48)],
            dst_ref=blocks.at[slot(2 * s + core)],
            send_sem=as_sem.at[s, c],
            recv_sem=ar_sem.at[2 * s + core],
            device_id={"outer": to}, device_id_type=MESH)

    def block_recv(m):
        return pltpu.make_async_remote_copy(
            src_ref=blocks.at[slot(m)], dst_ref=blocks.at[slot(m)], send_sem=as_sem.at[0, 0],
            recv_sem=ar_sem.at[m], device_id={"outer": owner(m)}, device_id_type=MESH)

    def peer_copy(h, i, m):
        start = k * rack_rows + (o ^ 1) * rows48
        return pltpu.make_async_remote_copy(
            src_ref=p.at[pl.ds(pl.multiple_of(start, 16), rows48), side(h, i)],
            dst_ref=blocks.at[slot(m), side(h, i)],
            send_sem=as_sem.at[i, h],
            recv_sem=ar_sem.at[n_outer + 2 * (i - 7) + h],
            device_id={"outer": o ^ 1}, device_id_type=MESH)

    def finish(i):
        s = pieces[i][0]
        for h, kinds in ((0, (1, 4)), (1, (3, 5))):
            for kind in kinds:
                message(kind, i).wait_recv()
            add_into(k, h, i, kinds)
            if s == 7:
                peer_copy(h, i, 14 + core).start()
        if s < 7:
            for c in range(2):
                block_send(s, c).start()
        else:
            start = pl.multiple_of(k * rack_rows + o * rows48, 16)
            for h in range(2):
                blocks[slot(14 + core), side(h, i)] = p[pl.ds(start, rows48), side(h, i)]

    def finish_last():
        first, size = pieces[9][1:]
        cols = pl.ds(first, size)
        mine = pl.ds(pl.multiple_of(core * rows48, 16), rows48)
        theirs = pl.ds(pl.multiple_of((1 - core) * rows48, 16), rows48)
        for h, kind in ((0, 1), (1, 3)):
            message(kind, 9).wait_recv()
            rows = rows_for(k, o ^ 1)
            total = p[rows, side(h, 9)].astype(F32) + xr[7, kind, theirs, cols].astype(F32)
            p[rows, side(h, 9)] = total.astype(BF16)
            peer_copy(h, 9, 14 + core).start()
        for h, kind in ((0, 1), (1, 3)):
            message(kind // 2 + 4, 9).wait_recv()
            total = p[rows_for(k, o), side(h, 9)].astype(F32)
            for part in (kind, kind // 2 + 4):
                total = total + xr[7, part, mine, cols].astype(F32)
            blocks[slot(14 + core), side(h, 9)] = total.astype(BF16)

    def gram(i):
        s, first = pieces[i][:2]
        if s < 7:
            for c in range(2):
                block_recv(2 * s + c).wait_recv()
        else:
            for h in range(2):
                for part in ((7,) if i == 7 else (8, 9)):
                    peer_copy(h, part, 15 - core).wait_recv()
                if i == 8:
                    passed(h).wait_recv()
                    here = slot(15 - core)
                    total = blocks[here, side(h, 9)].astype(F32) + xq[h].astype(F32)
                    blocks[here, side(h, 9)] = total.astype(BF16)
        count = 2 * s + 2
        newest = pl.ds(2 * s * rows48, step_rows)
        columns = (pl.ds(0, width),)
        if s == 7:
            size = cuts[1] if i == 7 else half - cuts[1]
            columns = tuple(pl.ds(h * half + first, size) for h in range(2))
        products = 0.0
        for cols in columns:
            products = products + lax.dot_general(
                blocks[pl.ds(0, count * rows48), cols], blocks[newest, cols],
                (((1,), (1,)), ((), ())), preferred_element_type=F32)
        row = lax.broadcasted_iota(jnp.int32, (count, rows48, step_rows), 1)
        lane = lax.broadcasted_iota(jnp.int32, (count, rows48, step_rows), 2)
        mask = (row == lane) | (row + rows48 == lane)
        trace = jnp.sum(
            jnp.where(mask, products.reshape(count, rows48, step_rows), 0.0), axis=1)
        if first > 0:
            trace = trace + lines[...]
        if i == 7:
            lines[...] = trace
            return
        lane = lax.broadcasted_iota(jnp.int32, (count, step_rows), 1)
        for a in range(2):
            new = owner(2 * s + a)
            mine = jnp.where(lane // rows48 == a, trace, 0.0)
            for m in range(count):
                pairs[new, pl.ds(owner(m), 1), :] = mine[m:m + 1]
                if m < 2 * s:
                    pairs[owner(m), pl.ds(new, 1), :] = mine[m:m + 1]

    cot_load(0).wait()
    ctx_load(0).wait()
    product(0, 0, 2, 0)
    pl.semaphore_wait(barrier, 7)
    opening(0, 0).start()
    ctx_load(1).wait()
    product(0, 1, 2, 0)
    opening(1, 0).start()
    product(0, 0, 2, 1)
    opening(0, 1).start()
    product(0, 1, 2, 1)
    opening(1, 1).start()
    greet(near_sem, adjacent)
    cot_load(2).wait()
    product(2, 1)
    message(3, 0).start()
    cot_load(1).wait()
    product(1, 0)
    message(1, 0).start()
    pl.semaphore_wait(near_sem, 6)
    greet(far_sem, second)
    cot_load(4).wait()
    product(4, 0)
    message(0, 1).start()
    product(4, 1)
    message(2, 1).start()
    product(2, 0)
    product(1, 1)
    relay(0)
    cot_load(6).wait()
    product(6, 1)
    message(3, 1).start()
    cot_load(5).wait()
    product(5, 0)
    message(1, 1).start()
    product(6, 0)
    product(5, 1)
    pl.semaphore_wait(far_sem, 5)
    greet(core_sem, [{"outer": o ^ 1}])
    first_hops(2)
    unit(3)
    unit(7)
    pl.semaphore_wait(core_sem, 1)
    for s in range(1, 7):
        relay(s)
        if s + 2 < 7:
            first_hops(s + 2)
        if s == 6:
            for kinds in ((0, 2), (3, 1)):
                for i in (7, 8, 9):
                    for kind in kinds:
                        message(kind, i).start()
        finish(s - 1)
        if s >= 3:
            gram(s - 3)
    finish(6)
    relay(7)
    gram(4)
    relay(8)
    relay(9)
    gram(5)
    finish(7)
    gram(6)
    finish(8)
    finish_last()
    gram(7)
    gram(8)

    rowsum = jnp.sum(pairs[...], axis=2, keepdims=True)
    j_index = lax.broadcasted_iota(jnp.int32, (n_outer, n_outer, 128), 1)
    lanes = lax.broadcasted_iota(jnp.int32, (n_outer, n_outer, 128), 2)
    me1 = k * n_tp + t
    g1[me1] = jnp.sum(jnp.where(j_index == lanes, rowsum, 0.0), axis=1)

    def share1(d):
        to_k, to_t = (k + d // n_tp) % n_rack, (t + d % n_tp) % n_tp
        return pltpu.make_async_remote_copy(
            src_ref=g1.at[me1], dst_ref=g1.at[me1], send_sem=gs_sem.at[0, d],
            recv_sem=gr_sem.at[0, me1], device_id={"rack": to_k, "tp": to_t}, device_id_type=MESH)

    def share1_recv(d):
        from_k, from_t = (k + d // n_tp) % n_rack, (t + d % n_tp) % n_tp
        q = from_k * n_tp + from_t
        return pltpu.make_async_remote_copy(
            src_ref=g1.at[q], dst_ref=g1.at[q], send_sem=gs_sem.at[0, d],
            recv_sem=gr_sem.at[0, q], device_id={"rack": from_k, "tp": from_t}, device_id_type=MESH)

    def hops(d):
        return min(d // n_tp, n_rack - d // n_tp) + min(d % n_tp, n_tp - d % n_tp)

    for d in sorted(range(1, n_rack * n_tp), key=hops, reverse=True):
        share1(d).start()
    for i in range(10):
        for kind in range(6):
            if i == 0 and kind in (0, 2):
                for c in range(2):
                    opening(kind // 2, c).wait_send()
            else:
                message(kind, i).wait_send()
        for h in range(2):
            if i < 7:
                block_send(i, h).wait_send()
            else:
                peer_copy(h, i, 14 + core).wait_send()
    for h in range(2):
        passed(h).wait_send()
    for d in range(1, n_rack * n_tp):
        share1_recv(d).wait_recv()
    g2[o] = jnp.sum(g1[...], axis=0)

    def share2(d):
        return pltpu.make_async_remote_copy(
            src_ref=g2.at[o], dst_ref=g2.at[o], send_sem=gs_sem.at[1, d],
            recv_sem=gr_sem.at[1, o], device_id={"outer": (o + d) % n_outer}, device_id_type=MESH)

    def share2_recv(d):
        q = (o + d) % n_outer
        return pltpu.make_async_remote_copy(
            src_ref=g2.at[q], dst_ref=g2.at[q], send_sem=gs_sem.at[1, d],
            recv_sem=gr_sem.at[1, q], device_id={"outer": q}, device_id_type=MESH)

    for d in sorted(range(1, n_outer), key=lambda d: abs(2 * d - n_outer)):
        share2(d).start()
    for d in range(1, n_outer):
        share2_recv(d).wait_recv()
    weights = merge_weights(jnp.sum(g2[...], axis=0), n_outer, 4)

    merged[...] = jnp.broadcast_to(weights, merged.shape)
    spread = [
        jnp.broadcast_to(merged[pl.ds(owner(m), 1), :], (16, 128)) for m in range(n_outer)]

    def out_copy(r):
        rows = pl.ds(r * 16, 16)
        return pltpu.make_async_copy(out.at[rows], out_hbm.at[rows], out_sem.at[r])

    for r in range(rows48 // 16):
        for c in range(width // 128):
            cols = pl.ds(c * 128, 128)
            total = 0.0
            for m in range(n_outer):
                rows = pl.ds(m * rows48 + r * 16, 16)
                total = total + spread[m] * blocks[rows, cols].astype(F32)
            out[pl.ds(r * 16, 16), cols] = total.astype(BF16)
        out_copy(r).start()
    for r in range(rows48 // 16):
        out_copy(r).wait()

    for d in range(1, n_rack * n_tp):
        share1(d).wait_send()
    for d in range(1, n_outer):
        share2(d).wait_send()


def shards(context, cotangent):
    tok, width = context.shape
    cols = cotangent.shape[1]
    n_outer = lax.axis_size("outer")
    rack_rows = cols // 4
    rows48 = rack_rows // 16
    return pl.pallas_call(
        kernel,
        out_shape=jax.ShapeDtypeStruct((rows48, width), BF16),
        in_specs=[pl.BlockSpec(memory_space=pl.ANY)] * 2,
        out_specs=pl.BlockSpec(memory_space=pl.ANY),
        scratch_shapes=[
            pltpu.VMEM((rows48, width), BF16),
            pltpu.VMEM((tok, width), BF16),
            pltpu.VMEM((8, tok, rack_rows // 2), BF16),
            pltpu.VMEM((cols, width), BF16),
            pltpu.VMEM((8, 6, 2 * rows48, width // 2), BF16),
            pltpu.VMEM((2, rows48, width // 12), BF16),
            pltpu.VMEM((n_outer * rows48, width), BF16),
            pltpu.VMEM((n_outer, n_outer, 2 * rows48), F32),
            pltpu.VMEM((n_outer, 2 * rows48), F32),
            pltpu.VMEM((n_outer, 128), F32),
            pltpu.VMEM((16, n_outer, 128), F32),
            pltpu.VMEM((16, n_outer, 128), F32),
            pltpu.SemaphoreType.DMA((10,)),
            pltpu.SemaphoreType.DMA((10, 6)),
            pltpu.SemaphoreType.DMA((10, 6)),
            pltpu.SemaphoreType.DMA((10, 2)),
            pltpu.SemaphoreType.DMA((22,)),
            pltpu.SemaphoreType.DMA((2, 16)),
            pltpu.SemaphoreType.DMA((2, 16)),
            pltpu.SemaphoreType.REGULAR,
            pltpu.SemaphoreType.REGULAR,
            pltpu.SemaphoreType.REGULAR,
            pltpu.SemaphoreType.DMA((rows48 // 16,)),
            pltpu.SemaphoreType.DMA((2,)),
            pltpu.SemaphoreType.DMA((2,)),
            pltpu.SemaphoreType.DMA((2, 2)),
            pltpu.SemaphoreType.DMA((2, 2)),
        ],
        compiler_params=pltpu.CompilerParams(
            collective_id=0, has_side_effects=True, vmem_limit_bytes=56 * 2**20),
    )(context, cotangent)


def solution(mesh):
    return jax.shard_map(
        shards,
        mesh=mesh,
        in_specs=(P(("rack", "outer"), "tp"), P(("rack", "outer"), None)),
        out_specs=P(("rack", "outer"), "tp"),
        check_vma=False,
    )
```

```python
import functools
import jax
import jax.numpy as jnp
from jax import lax
from jax.experimental import pallas as pl
from jax.experimental.pallas import tpu as pltpu
from jax.sharding import PartitionSpec as P

EPS = 1e-06
MESH = pl.DeviceIdType.MESH
F32 = jnp.float32
BF16 = jnp.bfloat16


def xor_roll(x, distance, axis, index, size):
    up = pltpu.roll(x, x.shape[axis] - distance, axis)
    down = pltpu.roll(x, distance, axis)
    return jnp.where((index & distance) == 0, up, down)


def merge_weights(gram, n, levels):
    row = lax.broadcasted_iota(jnp.int32, gram.shape, 0)
    lane = lax.broadcasted_iota(jnp.int32, gram.shape, 1)
    diagonal = row == lane
    weights_t = jnp.where(diagonal, 1.0, 0.0).astype(F32)

    def mixing(aa, bb, ab):
        aa, bb = jnp.maximum(aa, 0.0), jnp.maximum(bb, 0.0)
        bound = jnp.sqrt(aa) * jnp.sqrt(bb)
        ab = jnp.clip(ab, -bound, bound)
        return 1.0 - ab / (2.0 * (aa + EPS)), 1.0 - ab / (2.0 * (bb + EPS))

    for level in range(levels):
        d = 1 << level
        partner = (row ^ d) == lane
        gram_r = xor_roll(gram, d, 0, row, n)
        gram_l = xor_roll(gram, d, 1, lane, n)

        def column(x, mask):
            return jnp.sum(jnp.where(mask, x, 0.0), axis=1, keepdims=True)

        def line(x, mask):
            return jnp.sum(jnp.where(mask, x, 0.0), axis=0, keepdims=True)

        ca, cb = mixing(column(gram, diagonal), column(gram_r, partner), column(gram, partner))
        ra, rb = mixing(line(gram, diagonal), line(gram_l, partner), line(gram, partner))
        mixed = ca * gram + cb * gram_r
        gram = ra * mixed + rb * xor_roll(mixed, d, 1, lane, n)
        weights_t = ra * weights_t + rb * xor_roll(weights_t, d, 1, lane, n)
    return weights_t[:, 0:1]


def kernel(ctx_hbm, cot_hbm, out_hbm, out, ctx, cot, p, xr, xq, blocks, pairs, lines, merged, g1, g2,
           load_sem, xs_sem, xr_sem, as_sem, ar_sem, gs_sem, gr_sem, near_sem, far_sem, core_sem,
           out_sem, ps_sem, pr_sem, os_sem, or_sem):
    n_rack, n_outer, n_tp = lax.axis_size("rack"), lax.axis_size("outer"), lax.axis_size("tp")
    k, o, t = lax.axis_index("rack"), lax.axis_index("outer"), lax.axis_index("tp")
    left, right, opp = (k + 3) % 4, (k + 1) % 4, (k + 2) % 4
    z, core = o // 2, o % 2
    zh, zl = z // 4, z % 4
    tok, width = ctx.shape
    half = width // 2
    rack_rows = p.shape[0] // 4
    rows48 = rack_rows // 16
    step_rows = 2 * rows48
    unit_rows = rack_rows // 2
    dest = (opp, right, left, k)

    def along_z(d):
        return {"outer": (z + d) % 8 * 2 + core}

    adjacent = [{"rack": left}, {"rack": right}, {"tp": (t + 1) % 4}, {"tp": (t + 3) % 4},
                along_z(1), along_z(7)]
    second = [{"rack": left}, {"rack": right}, {"rack": opp}, along_z(2), along_z(6)]
    barrier = pltpu.get_barrier_semaphore()
    for device in adjacent + [{"outer": o ^ 1}]:
        pl.semaphore_signal(barrier, inc=1, device_id=device, device_id_type=MESH)

    def greet(semaphore, devices):
        for device in devices:
            pl.semaphore_signal(semaphore, inc=1, device_id=device, device_id_type=MESH)

    def distance(s):
        odd = s % 2
        return (1 - odd) * (4 + s // 2) + odd * ((7 - s) // 2)

    def target(s):
        return (z + distance(s)) % 8

    def source(s):
        return (z + 8 - distance(s)) % 8

    def unit_cols(u):
        h = zh ^ (1 - u // 4)
        return dest[u % 4] * rack_rows + h * unit_rows

    def cot_load(u):
        cols = pl.ds(pl.multiple_of(unit_cols(u), 128), unit_rows)
        return pltpu.make_async_copy(cot_hbm.at[:, cols], cot.at[u], load_sem.at[u])

    def ctx_load(h):
        cols = pl.ds(h * half, half)
        return pltpu.make_async_copy(ctx_hbm.at[:, cols], ctx.at[:, cols], load_sem.at[8 + h])

    cot_load(0).start()
    for h in range(2):
        ctx_load(h).start()
    for u in range(1, 8):
        cot_load(u).start()

    def product(u, h, parts=1, part=0):
        size = half // parts
        cols = pl.ds(pl.multiple_of(h * half + part * size, size), size)
        p[pl.ds(pl.multiple_of(unit_cols(u), 128), unit_rows), cols] = lax.dot_general(
            cot[u], ctx[:, cols], (((0,), (0,)), ((), ())),
            preferred_element_type=F32).astype(BF16)

    def unit(u):
        cot_load(u).wait()

        @pl.loop(0, 2)
        def _(h):
            product(u, h)

    lane_tiles = half // 128
    cuts = (0, lane_tiles // 2 * 128, lane_tiles * 5 // 6 * 128, half)
    pieces = [(s, 0, half) for s in range(7)]
    pieces += [(7, cuts[i], cuts[i + 1] - cuts[i]) for i in range(3)]

    def side(h, i):
        _, first, size = pieces[i]
        return pl.ds(h * half + first, size)

    def rows_of(j, s):
        return pl.ds(pl.multiple_of(j * rack_rows + target(s) * step_rows, 16), step_rows)

    def rows_for(j, group):
        return pl.ds(pl.multiple_of(j * rack_rows + group * rows48, 16), rows48)

    def message(kind, i):
        s, first, size = pieces[i]
        j, h, to = (
            (opp, 0, left), (right, 0, right), (opp, 1, right), (left, 1, left),
            (left, 0, left), (right, 1, right))[kind]
        rows, there = rows_of(j, s), pl.ds(0, step_rows)
        if i == 9 and kind >= 4:
            rows, there = rows_for(j, o), pl.ds(pl.multiple_of(core * rows48, 16), rows48)
        return pltpu.make_async_remote_copy(
            src_ref=p.at[rows, side(h, i)],
            dst_ref=xr.at[s, kind, there, pl.ds(first, size)],
            send_sem=xs_sem.at[i, kind],
            recv_sem=xr_sem.at[i, kind],
            device_id={"rack": to}, device_id_type=MESH)

    def passed(h):
        j = (left, right)[h]
        return pltpu.make_async_remote_copy(
            src_ref=p.at[rows_for(j, o ^ 1), side(h, 9)],
            dst_ref=xq.at[h],
            send_sem=ps_sem.at[h],
            recv_sem=pr_sem.at[h],
            device_id={"rack": j, "outer": o ^ 1}, device_id_type=MESH)

    def add_into(j, h, i, kinds):
        s, first, size = pieces[i]
        rows = rows_of(j, s)

        @pl.loop(0, step_rows // 16)
        def _(r):
            here = pl.ds(pl.multiple_of(rows.start + r * 16, 16), 16)
            there = pl.ds(pl.multiple_of(r * 16, 16), 16)
            total = p[here, side(h, i)].astype(F32)
            for kind in kinds:
                total = total + xr[s, kind, there, pl.ds(first, size)].astype(F32)
            p[here, side(h, i)] = total.astype(BF16)

    def opening(h, c):
        cols = pl.ds(c * (half // 2), half // 2)
        return pltpu.make_async_remote_copy(
            src_ref=p.at[rows_of(opp, 0), pl.ds(h * half + c * (half // 2), half // 2)],
            dst_ref=xr.at[0, 2 * h, :, cols],
            send_sem=os_sem.at[h, c],
            recv_sem=or_sem.at[h, c],
            device_id={"rack": (left, right)[h]}, device_id_type=MESH)

    def arrived(h, i):
        if i == 0:
            for c in range(2):
                opening(h, c).wait_recv()
        else:
            message(2 * h, i).wait_recv()

    def first_hops(i):
        for kind in (0, 2, 3, 1):
            message(kind, i).start()

    def relay(i):
        arrived(0, i)
        add_into(left, 0, i, (0,))
        message(4, i).start()
        if i == 9:
            passed(0).start()
        arrived(1, i)
        add_into(right, 1, i, (2,))
        message(5, i).start()
        if i == 9:
            passed(1).start()

    def slot(m):
        return pl.ds(pl.multiple_of(m * rows48, 16), rows48)

    def owner(m):
        return source(m // 2) * 2 + m % 2

    def block_send(s, c):
        to = target(s) * 2 + c
        start = k * rack_rows + target(s) * step_rows + c * rows48
        return pltpu.make_async_remote_copy(
            src_ref=p.at[pl.ds(pl.multiple_of(start, 16), rows48)],
            dst_ref=blocks.at[slot(2 * s + core)],
            send_sem=as_sem.at[s, c],
            recv_sem=ar_sem.at[2 * s + core],
            device_id={"outer": to}, device_id_type=MESH)

    def block_recv(m):
        return pltpu.make_async_remote_copy(
            src_ref=blocks.at[slot(m)], dst_ref=blocks.at[slot(m)], send_sem=as_sem.at[0, 0],
            recv_sem=ar_sem.at[m], device_id={"outer": owner(m)}, device_id_type=MESH)

    def peer_copy(h, i, m):
        start = k * rack_rows + (o ^ 1) * rows48
        return pltpu.make_async_remote_copy(
            src_ref=p.at[pl.ds(pl.multiple_of(start, 16), rows48), side(h, i)],
            dst_ref=blocks.at[slot(m), side(h, i)],
            send_sem=as_sem.at[i, h],
            recv_sem=ar_sem.at[n_outer + 2 * (i - 7) + h],
            device_id={"outer": o ^ 1}, device_id_type=MESH)

    def finish(i):
        s = pieces[i][0]
        for h, kinds in ((0, (1, 4)), (1, (3, 5))):
            for kind in kinds:
                message(kind, i).wait_recv()
            add_into(k, h, i, kinds)
            if s == 7:
                peer_copy(h, i, 14 + core).start()
        if s < 7:
            for c in range(2):
                block_send(s, c).start()
        else:
            start = pl.multiple_of(k * rack_rows + o * rows48, 16)
            for h in range(2):
                blocks[slot(14 + core), side(h, i)] = p[pl.ds(start, rows48), side(h, i)]

    def finish_last():
        first, size = pieces[9][1:]
        cols = pl.ds(first, size)
        mine = pl.ds(pl.multiple_of(core * rows48, 16), rows48)
        theirs = pl.ds(pl.multiple_of((1 - core) * rows48, 16), rows48)
        for h, kind in ((0, 1), (1, 3)):
            message(kind, 9).wait_recv()
            rows = rows_for(k, o ^ 1)
            total = p[rows, side(h, 9)].astype(F32) + xr[7, kind, theirs, cols].astype(F32)
            p[rows, side(h, 9)] = total.astype(BF16)
            peer_copy(h, 9, 14 + core).start()
        for h, kind in ((0, 1), (1, 3)):
            message(kind // 2 + 4, 9).wait_recv()
            total = p[rows_for(k, o), side(h, 9)].astype(F32)
            for part in (kind, kind // 2 + 4):
                total = total + xr[7, part, mine, cols].astype(F32)
            blocks[slot(14 + core), side(h, 9)] = total.astype(BF16)

    def gram(i):
        s, first = pieces[i][:2]
        if s < 7:
            for c in range(2):
                block_recv(2 * s + c).wait_recv()
        else:
            for h in range(2):
                for part in ((7,) if i == 7 else (8, 9)):
                    peer_copy(h, part, 15 - core).wait_recv()
                if i == 8:
                    passed(h).wait_recv()
                    here = slot(15 - core)
                    total = blocks[here, side(h, 9)].astype(F32) + xq[h].astype(F32)
                    blocks[here, side(h, 9)] = total.astype(BF16)
        count = 2 * s + 2
        newest = pl.ds(2 * s * rows48, step_rows)
        columns = (pl.ds(0, width),)
        if s == 7:
            size = cuts[1] if i == 7 else half - cuts[1]
            columns = tuple(pl.ds(h * half + first, size) for h in range(2))
        products = 0.0
        for cols in columns:
            products = products + lax.dot_general(
                blocks[pl.ds(0, count * rows48), cols], blocks[newest, cols],
                (((1,), (1,)), ((), ())), preferred_element_type=F32)
        row = lax.broadcasted_iota(jnp.int32, (count, rows48, step_rows), 1)
        lane = lax.broadcasted_iota(jnp.int32, (count, rows48, step_rows), 2)
        mask = (row == lane) | (row + rows48 == lane)
        trace = jnp.sum(
            jnp.where(mask, products.reshape(count, rows48, step_rows), 0.0), axis=1)
        if first > 0:
            trace = trace + lines[...]
        if i == 7:
            lines[...] = trace
            return
        lane = lax.broadcasted_iota(jnp.int32, (count, step_rows), 1)
        for a in range(2):
            new = owner(2 * s + a)
            mine = jnp.where(lane // rows48 == a, trace, 0.0)
            for m in range(count):
                pairs[new, pl.ds(owner(m), 1), :] = mine[m:m + 1]
                if m < 2 * s:
                    pairs[owner(m), pl.ds(new, 1), :] = mine[m:m + 1]

    cot_load(0).wait()
    ctx_load(0).wait()
    product(0, 0, 2, 0)
    pl.semaphore_wait(barrier, 7)
    opening(0, 0).start()
    ctx_load(1).wait()
    product(0, 1, 2, 0)
    opening(1, 0).start()
    product(0, 0, 2, 1)
    opening(0, 1).start()
    product(0, 1, 2, 1)
    opening(1, 1).start()
    greet(near_sem, adjacent)
    cot_load(2).wait()
    product(2, 1)
    message(3, 0).start()
    cot_load(1).wait()
    product(1, 0)
    message(1, 0).start()
    pl.semaphore_wait(near_sem, 6)
    greet(far_sem, second)
    cot_load(4).wait()
    product(4, 0)
    message(0, 1).start()
    product(4, 1)
    message(2, 1).start()
    product(2, 0)
    product(1, 1)
    relay(0)
    cot_load(6).wait()
    product(6, 1)
    message(3, 1).start()
    cot_load(5).wait()
    product(5, 0)
    message(1, 1).start()
    product(6, 0)
    product(5, 1)
    pl.semaphore_wait(far_sem, 5)
    greet(core_sem, [{"outer": o ^ 1}])
    first_hops(2)
    unit(3)
    unit(7)
    pl.semaphore_wait(core_sem, 1)
    for s in range(1, 7):
        relay(s)
        if s + 2 < 7:
            first_hops(s + 2)
        if s == 6:
            for kinds in ((0, 2), (3, 1)):
                for i in (7, 8, 9):
                    for kind in kinds:
                        message(kind, i).start()
        finish(s - 1)
        if s >= 3:
            gram(s - 3)
    finish(6)
    relay(7)
    gram(4)
    relay(8)
    relay(9)
    finish(7)
    gram(5)
    gram(6)
    finish(8)
    finish_last()
    gram(7)
    gram(8)

    rowsum = jnp.sum(pairs[...], axis=2, keepdims=True)
    j_index = lax.broadcasted_iota(jnp.int32, (n_outer, n_outer, 128), 1)
    lanes = lax.broadcasted_iota(jnp.int32, (n_outer, n_outer, 128), 2)
    me1 = k * n_tp + t
    g1[me1] = jnp.sum(jnp.where(j_index == lanes, rowsum, 0.0), axis=1)

    def share1(d):
        to_k, to_t = (k + d // n_tp) % n_rack, (t + d % n_tp) % n_tp
        return pltpu.make_async_remote_copy(
            src_ref=g1.at[me1], dst_ref=g1.at[me1], send_sem=gs_sem.at[0, d],
            recv_sem=gr_sem.at[0, me1], device_id={"rack": to_k, "tp": to_t}, device_id_type=MESH)

    def share1_recv(d):
        from_k, from_t = (k + d // n_tp) % n_rack, (t + d % n_tp) % n_tp
        q = from_k * n_tp + from_t
        return pltpu.make_async_remote_copy(
            src_ref=g1.at[q], dst_ref=g1.at[q], send_sem=gs_sem.at[0, d],
            recv_sem=gr_sem.at[0, q], device_id={"rack": from_k, "tp": from_t}, device_id_type=MESH)

    def hops(d):
        return min(d // n_tp, n_rack - d // n_tp) + min(d % n_tp, n_tp - d % n_tp)

    for d in sorted(range(1, n_rack * n_tp), key=hops, reverse=True):
        share1(d).start()
    for i in range(10):
        for kind in range(6):
            if i == 0 and kind in (0, 2):
                for c in range(2):
                    opening(kind // 2, c).wait_send()
            else:
                message(kind, i).wait_send()
        for h in range(2):
            if i < 7:
                block_send(i, h).wait_send()
            else:
                peer_copy(h, i, 14 + core).wait_send()
    for h in range(2):
        passed(h).wait_send()
    for d in range(1, n_rack * n_tp):
        share1_recv(d).wait_recv()
    g2[o] = jnp.sum(g1[...], axis=0)

    def share2(d):
        return pltpu.make_async_remote_copy(
            src_ref=g2.at[o], dst_ref=g2.at[o], send_sem=gs_sem.at[1, d],
            recv_sem=gr_sem.at[1, o], device_id={"outer": (o + d) % n_outer}, device_id_type=MESH)

    def share2_recv(d):
        q = (o + d) % n_outer
        return pltpu.make_async_remote_copy(
            src_ref=g2.at[q], dst_ref=g2.at[q], send_sem=gs_sem.at[1, d],
            recv_sem=gr_sem.at[1, q], device_id={"outer": q}, device_id_type=MESH)

    for d in sorted(range(1, n_outer), key=lambda d: abs(2 * d - n_outer)):
        share2(d).start()
    for d in range(1, n_outer):
        share2_recv(d).wait_recv()
    weights = merge_weights(jnp.sum(g2[...], axis=0), n_outer, 4)

    merged[...] = jnp.broadcast_to(weights, merged.shape)
    spread = [
        jnp.broadcast_to(merged[pl.ds(owner(m), 1), :], (16, 128)) for m in range(n_outer)]

    def out_copy(r):
        rows = pl.ds(r * 16, 16)
        return pltpu.make_async_copy(out.at[rows], out_hbm.at[rows], out_sem.at[r])

    for r in range(rows48 // 16):
        for c in range(width // 128):
            cols = pl.ds(c * 128, 128)
            total = 0.0
            for m in range(n_outer):
                rows = pl.ds(m * rows48 + r * 16, 16)
                total = total + spread[m] * blocks[rows, cols].astype(F32)
            out[pl.ds(r * 16, 16), cols] = total.astype(BF16)
        out_copy(r).start()
    for r in range(rows48 // 16):
        out_copy(r).wait()

    for d in range(1, n_rack * n_tp):
        share1(d).wait_send()
    for d in range(1, n_outer):
        share2(d).wait_send()


def shards(context, cotangent):
    tok, width = context.shape
    cols = cotangent.shape[1]
    n_outer = lax.axis_size("outer")
    rack_rows = cols // 4
    rows48 = rack_rows // 16
    return pl.pallas_call(
        kernel,
        out_shape=jax.ShapeDtypeStruct((rows48, width), BF16),
        in_specs=[pl.BlockSpec(memory_space=pl.ANY)] * 2,
        out_specs=pl.BlockSpec(memory_space=pl.ANY),
        scratch_shapes=[
            pltpu.VMEM((rows48, width), BF16),
            pltpu.VMEM((tok, width), BF16),
            pltpu.VMEM((8, tok, rack_rows // 2), BF16),
            pltpu.VMEM((cols, width), BF16),
            pltpu.VMEM((8, 6, 2 * rows48, width // 2), BF16),
            pltpu.VMEM((2, rows48, width // 12), BF16),
            pltpu.VMEM((n_outer * rows48, width), BF16),
            pltpu.VMEM((n_outer, n_outer, 2 * rows48), F32),
            pltpu.VMEM((n_outer, 2 * rows48), F32),
            pltpu.VMEM((n_outer, 128), F32),
            pltpu.VMEM((16, n_outer, 128), F32),
            pltpu.VMEM((16, n_outer, 128), F32),
            pltpu.SemaphoreType.DMA((10,)),
            pltpu.SemaphoreType.DMA((10, 6)),
            pltpu.SemaphoreType.DMA((10, 6)),
            pltpu.SemaphoreType.DMA((10, 2)),
            pltpu.SemaphoreType.DMA((22,)),
            pltpu.SemaphoreType.DMA((2, 16)),
            pltpu.SemaphoreType.DMA((2, 16)),
            pltpu.SemaphoreType.REGULAR,
            pltpu.SemaphoreType.REGULAR,
            pltpu.SemaphoreType.REGULAR,
            pltpu.SemaphoreType.DMA((rows48 // 16,)),
            pltpu.SemaphoreType.DMA((2,)),
            pltpu.SemaphoreType.DMA((2,)),
            pltpu.SemaphoreType.DMA((2, 2)),
            pltpu.SemaphoreType.DMA((2, 2)),
        ],
        compiler_params=pltpu.CompilerParams(
            collective_id=0, has_side_effects=True, vmem_limit_bytes=56 * 2**20),
    )(context, cotangent)


def solution(mesh):
    return jax.shard_map(
        shards,
        mesh=mesh,
        in_specs=(P(("rack", "outer"), "tp"), P(("rack", "outer"), None)),
        out_specs=P(("rack", "outer"), "tp"),
        check_vma=False,
    )
```
